256 devices in a mesh: dp: 16 (over z, core), slab: 4 (over x), fsdp: 4 (over y).
Axes of the slice: x: 4, y: 4, z: 8, core: 2. Of those that a mesh axis runs over, the one named last changes fastest.
Arguments:
- pixels: bfloat16 [16, 4, 16, 3, 224, 224], P('dp', 'fsdp', 'slab'), may hold values from -6 to 6
- grad_norm: bfloat16 [4, 4, 8192, 1280], P('slab', 'fsdp', 'dp'), may hold values from -0.015625 to 0.015625
- grad_resid: bfloat16 [4, 4, 8192, 1280], P('slab', 'fsdp', 'dp'), may hold values from -0.015625 to 0.015625
- embed_weight: bfloat16 [1280, 1176], P('fsdp'), may hold values from -0.1875 to 0.1875
- norm_gain: float32 [1280], replicated, may hold values from 0.1 to 1.9
- send_slot: int32 [4, 4, 8192], P('slab', 'fsdp', 'dp'), may hold values from 0 to 1023, as said below
- recv_slot: int32 [4, 4, 8192], P('slab', 'fsdp', 'dp'), may hold values from 0 to 1023, as said below
Outputs:
- embed_grad: float32 [1280, 1176], P('fsdp')
- norm_grad: float32 [2, 1280], P(None, 'fsdp')
The draws below stay inside these ranges and needn't reach their ends.
Inputs may be any that keep to these rules, and one draw needn't show every extreme that they name: `send_slot`: within each slab and fsdp index, the rows of the dp group are a one-to-one map onto the tokens of the group's slab owners: each device sends all its 512 rows and its tokens receive exactly 512; the ranks of the rows from one device to one device run from 0 up without gaps; at most 64 rows go from one device to one device, and that many do in every draw. `recv_slot`: the inverse of send_slot: the values of one device are distinct and name each row that is sent to it exactly once.
All inputs are finite; a program needn't handle non-finite values.
Results may differ from the reference program's by a relative error of at most 0.0029.
Values may be sent and summed in bfloat16 or wider, within the bound.
No kernel may reach another device: no remote copies, remote signals or barrier semaphores. Data moves between devices by JAX's collectives and lax.ppermute only.
A program may use at most 128 MiB of HBM per device.

```python
import jax
import jax.numpy as jnp
from jax import lax

D = 1280
PATCH = 14
KIN = 1176
GH = 16
GW = 16
ROWS = 512
CAP = 64
FRAMES = 16
HEIGHT = 224
WIDTH_PX = 224
TOKENS = 131072
N_DP = 16
N_SLAB = 4
N_FSDP = 4


def number_rows(counts, key):
    ends = jnp.cumsum(counts, axis=1).astype(jnp.int32)
    starts = (ends - counts).astype(jnp.int32)
    places = jnp.arange(ROWS, dtype=jnp.int32)
    peers = jnp.sum((places[None, :, None] >= ends[:, None, :]).astype(jnp.int32), axis=2).astype(jnp.int32)
    ranks = places[None, :] - jnp.take_along_axis(starts, peers, axis=1)
    values = (peers * CAP + ranks).astype(jnp.int32)
    orders = jax.vmap(lambda k: jax.random.permutation(k, ROWS).astype(jnp.int32))(jax.random.split(key, N_DP))
    placed = jax.vmap(lambda o, v: jnp.zeros((ROWS,), jnp.int32).at[o].set(v))(orders, values)
    return placed.reshape(N_DP * ROWS)


def group_slots(key):
    key_spread, key_first, key_second, key_send, key_recv = jax.random.split(key, 5)
    middle = ROWS // N_DP
    spreads = jax.random.randint(key_spread, (N_DP // 2 - 1,), 0, middle + 1).astype(jnp.int32)
    paired = jnp.stack([middle + spreads, middle - spreads], axis=1).reshape(-1)
    levels = jnp.concatenate([jnp.array([2 * middle, 0], jnp.int32), paired.astype(jnp.int32)])
    first = jax.random.permutation(key_first, N_DP).astype(jnp.int32)
    second = jax.random.permutation(key_second, N_DP).astype(jnp.int32)
    counts = levels[(first[:, None] + second[None, :]) % N_DP].astype(jnp.int32)
    return (number_rows(counts, key_send), number_rows(counts.T, key_recv))


def slot_tables(key):
    keys = jax.random.split(key, N_SLAB * N_FSDP)
    sends, takes = jax.vmap(group_slots)(keys)
    return (sends.reshape(N_SLAB, N_FSDP, N_DP * ROWS), takes.reshape(N_SLAB, N_FSDP, N_DP * ROWS))


def draw_send_slot(key, part):
    return slot_tables(key)[0]


def draw_recv_slot(key, part):
    return slot_tables(key)[1]


def shard_levels(rng, dims, pieces, low, largest):
    gain = 1.0
    for axis_at, blocks in pieces:
        heights = jax.random.uniform(jax.random.fold_in(jax.random.fold_in(rng, 6), axis_at), (blocks,), jnp.float32, low / len(pieces), largest / len(pieces))
        gain = gain * jnp.repeat(jnp.exp(heights), dims[axis_at] // blocks).reshape((-1,) + (1,) * (len(dims) - 1 - axis_at))
    return gain


def bell_draw(rng, extent, scale, most, pieces=(), kind=jnp.bfloat16):
    level = shard_levels(rng, extent, pieces, -0.22, 0.18) if pieces else 1.0
    drawn = jax.random.normal(rng, extent, jnp.float32) * scale * level
    return jnp.minimum(jnp.maximum(drawn, -most), most).astype(kind)


def setup_inputs(seed: int = 0) -> dict:
    streams_of = jax.random.split(jax.random.key(seed), 8)
    return {
        "pixels": bell_draw(streams_of[0], (N_DP, N_FSDP, FRAMES, 3, HEIGHT, WIDTH_PX), 1.0, 6.0, ((0, 16), (1, 4), (2, 4))),
        "grad_norm": bell_draw(streams_of[1], (N_SLAB, N_FSDP, N_DP * ROWS, D), TOKENS ** -0.5, 0.015625, ((0, 4), (1, 4), (2, 16))),
        "grad_resid": bell_draw(streams_of[2], (N_SLAB, N_FSDP, N_DP * ROWS, D), TOKENS ** -0.5, 0.015625, ((0, 4), (1, 4), (2, 16))),
        "embed_weight": bell_draw(streams_of[3], (D, KIN), KIN ** -0.5, 0.1875, ((0, 4),)),
        "norm_gain": jnp.clip(1.0 + 0.18 * jax.random.normal(streams_of[4], (D,), jnp.float32), 0.1, 1.9),
        "send_slot": draw_send_slot(jax.random.fold_in(streams_of[7], 71), 0),
        "recv_slot": draw_recv_slot(jax.random.fold_in(streams_of[7], 71), 0),
    }


def patch_rows(frames):
    blank = jnp.zeros((1,) + frames.shape[1:], frames.dtype)
    shifted = jnp.concatenate([blank, frames[:-1]], axis=0)
    paired = shifted.reshape(FRAMES // 2, 2, 3, GH, PATCH, GW, PATCH)
    ordered = jnp.transpose(paired, (0, 3, 5, 2, 1, 4, 6))
    return ordered.reshape(FRAMES // 2 * GH * GW, KIN)

def norm_backward(patches, grad_rows, resid_rows, embed_weight, norm_gain):
    embedded = jnp.dot(patches, embed_weight.T, preferred_element_type=jnp.float32)
    center = lax.optimization_barrier(jnp.mean(embedded, axis=-1, keepdims=True))
    deviation = embedded - center
    variance = lax.optimization_barrier(jnp.mean(deviation * deviation, axis=-1, keepdims=True))
    inverse_std = lax.rsqrt(variance + 1e-06)
    normalized = deviation * inverse_std
    upstream_norm = grad_rows.astype(jnp.float32)
    upstream = upstream_norm * norm_gain
    inner = lax.optimization_barrier(jnp.mean(upstream * normalized, axis=-1, keepdims=True))
    input_grad = resid_rows.astype(jnp.float32) + inverse_std * (upstream - lax.optimization_barrier(jnp.mean(upstream, axis=-1, keepdims=True)) - normalized * inner)
    input_grad = input_grad.astype(jnp.bfloat16)
    weight_part = jnp.dot(input_grad.T, patches, preferred_element_type=jnp.float32)
    gain_part = lax.optimization_barrier(jnp.sum(upstream_norm * normalized, axis=0))
    bias_part = lax.optimization_barrier(jnp.sum(upstream_norm, axis=0))
    return (weight_part, gain_part, bias_part)

def reference(pixels, grad_norm, grad_resid, embed_weight, norm_gain, send_slot, recv_slot):
    videos = jax.vmap(jax.vmap(patch_rows))(pixels)
    total_rows = N_DP * ROWS

    def one_group(index):
        slab_index = index // N_FSDP
        fsdp_index = index % N_FSDP
        both = jnp.concatenate([grad_norm[slab_index, fsdp_index], grad_resid[slab_index, fsdp_index]], axis=1)
        slots = send_slot[slab_index, fsdp_index].astype(jnp.int32)
        sender = (jnp.arange(total_rows, dtype=jnp.int32) // ROWS).astype(jnp.int32)
        place = slots // CAP * (N_DP * CAP) + sender * CAP + slots % CAP
        table = jnp.zeros((N_DP * N_DP * CAP, 2 * D), jnp.bfloat16).at[place].set(both)
        owner = sender
        wanted = owner * (N_DP * CAP) + recv_slot[slab_index, fsdp_index].astype(jnp.int32)
        routed = table[wanted]
        group_videos = jnp.take(videos, fsdp_index, axis=1)
        patches = lax.dynamic_slice_in_dim(group_videos, (slab_index * ROWS).astype(jnp.int32), ROWS, axis=1)
        patches = patches.reshape(total_rows, KIN)
        return norm_backward(patches, routed[:, :D], routed[:, D:], embed_weight, norm_gain)
    weight_parts, gain_parts, bias_parts = lax.map(one_group, jnp.arange(N_SLAB * N_FSDP, dtype=jnp.int32))
    embed_grad = lax.optimization_barrier(jnp.sum(weight_parts, axis=0))
    norm_grad = jnp.stack([lax.optimization_barrier(jnp.sum(gain_parts, axis=0)), lax.optimization_barrier(jnp.sum(bias_parts, axis=0))], axis=0)
    return (embed_grad, norm_grad)
```

```python
import functools

import jax
import jax.numpy as jnp
import numpy as np
from jax import lax
from jax.experimental import pallas as pl
from jax.experimental.pallas import tpu as pltpu
from jax.sharding import Mesh
from jax.sharding import PartitionSpec as P

GH = 16
GW = 16
PS = 14
COLOURS = 3
SIDE = 224
ROWS = 512
CAP = 64
D = 1280
KIN = 1176
GROUPS = 9
PARTS = COLOURS * PS
HALF = 640
SUMS = 4 * 128 + 96
VMEM = 60 * 1024 * 1024


def column_places():
    place = np.zeros((1, KIN), np.int32)
    for c in range(COLOURS):
        for t in range(2):
            for p in range(PS):
                part = c * PS + p
                start = (1 - t) * HALF + part // GROUPS * 128 + part % GROUPS * PS
                at = (c * 2 + t) * PS * PS + p * PS
                place[0, at : at + PS] = start + np.arange(PS)
    return place


def div14(v):
    return (v * 4682) >> 16


def patch_kernel(slot_ref, fa_ref, fb_ref, out_ref, spread_ref, rows_ref):
    src = lax.broadcasted_iota(jnp.int32, (SIDE, 256), 0)
    dst = lax.broadcasted_iota(jnp.int32, (SIDE, 256), 1)
    place = jnp.where(src >= GROUPS * PS, src + 2, src)
    spread = (dst == place).astype(jnp.float32).astype(jnp.bfloat16)
    dst = lax.broadcasted_iota(jnp.int32, (SIDE, SIDE), 0)
    src = lax.broadcasted_iota(jnp.int32, (SIDE, SIDE), 1)
    regroup = (src == (dst & 15) * PS + (dst >> 4)).astype(jnp.float32).astype(jnp.bfloat16)
    for k, ref in enumerate((fa_ref, fb_ref)):
        for c in range(COLOURS):
            frame = ref[0, 0, 0, c]
            wide = jnp.dot(frame, spread, preferred_element_type=jnp.float32).astype(jnp.bfloat16)
            spread_ref[k, c] = jnp.dot(regroup, wide, preferred_element_type=jnp.float32)
    lane = lax.broadcasted_iota(jnp.int32, (GH, 128), 1)
    for k in range(2):
        for x in range(GW):
            tile = x // GROUPS * 128
            for j in range(5):
                acc = None
                used = min(GROUPS, PARTS - j * GROUPS)
                for a in range(used):
                    c, p = divmod(j * GROUPS + a, PS)
                    piece = spread_ref[k, c, p * GH : (p + 1) * GH, tile : tile + 128]
                    shift = PS * (a - x % GROUPS) % 128
                    if shift:
                        piece = pltpu.roll(piece, shift, 1)
                    acc = piece if acc is None else jnp.where(lane >= a * PS, piece, acc)
                acc = jnp.where(lane < used * PS, acc, 0.0)
                start = k * GH * GW + x * GH
                rows_ref[start : start + GH, j * 128 : (j + 1) * 128] = acc.astype(jnp.bfloat16)
    slots = slot_ref[...]

    def scatter(i, carry):
        start = pl.multiple_of(i * 256, 256)
        at = lax.broadcasted_iota(jnp.int32, (256, ROWS), 0) + start
        pick = (at == slots).astype(jnp.float32).astype(jnp.bfloat16)
        packed = jnp.dot(pick, rows_ref[...], preferred_element_type=jnp.float32)
        out_ref[pl.ds(start, 256), :] = packed.astype(jnp.bfloat16)
        return carry

    lax.fori_loop(0, 4, scatter, 0)


def packed_rows(slots, first, second, first_at, second_at):
    block = (1, 1, 1, COLOURS, SIDE, SIDE)
    return pl.pallas_call(
        patch_kernel,
        out_shape=jax.ShapeDtypeStruct((16 * CAP, HALF), jnp.bfloat16),
        grid=(1,),
        in_specs=[
            pl.BlockSpec((1, ROWS), lambda i: (0, 0)),
            pl.BlockSpec(block, lambda i: (0, 0, first_at, 0, 0, 0)),
            pl.BlockSpec(block, lambda i: (0, 0, second_at, 0, 0, 0)),
        ],
        out_specs=pl.BlockSpec((16 * CAP, HALF), lambda i: (0, 0)),
        scratch_shapes=[
            pltpu.VMEM((2, COLOURS, SIDE, 256), jnp.float32),
            pltpu.VMEM((ROWS, HALF), jnp.bfloat16),
        ],
        compiler_params=pltpu.CompilerParams(vmem_limit_bytes=VMEM),
        name="patch_rows",
    )(slots, first, second)


def weight_kernel(place_ref, w_ref, out_ref):
    place = place_ref[...]
    at = lax.broadcasted_iota(jnp.int32, (256, KIN), 0) + pl.program_id(0) * 256
    pick = (at == place).astype(jnp.float32).astype(jnp.bfloat16)
    out_ref[...] = lax.dot_general(
        pick, w_ref[...], (((1,), (1,)), ((), ())), preferred_element_type=jnp.float32
    ).astype(jnp.bfloat16)


def padded_weight(weight):
    return pl.pallas_call(
        weight_kernel,
        out_shape=jax.ShapeDtypeStruct((2 * HALF, D), jnp.bfloat16),
        grid=(5,),
        in_specs=[
            pl.BlockSpec((1, KIN), lambda i: (0, 0)),
            pl.BlockSpec((D, KIN), lambda i: (0, 0)),
        ],
        out_specs=pl.BlockSpec((256, D), lambda i: (i, 0)),
        compiler_params=pltpu.CompilerParams(vmem_limit_bytes=VMEM),
        name="weight_columns",
    )(jnp.asarray(column_places()), weight)


def backward_kernel(core_ref, slot_ref, arr0_ref, arr1_ref, w_ref, g_ref, r_ref, gain_ref, send_ref, keep_ref, rows_ref, grad_ref, sums_ref):
    gain = gain_ref[...]
    sums_ref[...] = jnp.zeros_like(sums_ref)

    def block(i, carry):
        start = pl.multiple_of(i * 128, 128)
        here = pl.ds(start, 128)
        at = lax.broadcasted_iota(jnp.int32, (128, 16 * CAP), 1)
        pick = (at == slot_ref[here, :]).astype(jnp.float32).astype(jnp.bfloat16)
        row0 = jnp.dot(pick, arr0_ref[...], preferred_element_type=jnp.float32).astype(jnp.bfloat16)
        row1 = jnp.dot(pick, arr1_ref[...], preferred_element_type=jnp.float32).astype(jnp.bfloat16)
        rows_ref[0, here, :] = row0
        rows_ref[1, here, :] = row1
        embedded = jnp.dot(row0, w_ref[:HALF, :], preferred_element_type=jnp.float32)
        embedded += jnp.dot(row1, w_ref[HALF:, :], preferred_element_type=jnp.float32)
        center = jnp.mean(embedded, axis=-1, keepdims=True)
        deviation = embedded - center
        variance = jnp.mean(deviation * deviation, axis=-1, keepdims=True)
        inverse_std = lax.rsqrt(variance + 1e-06)
        normalized = deviation * inverse_std
        upstream_norm = g_ref[0, 0, here, :].astype(jnp.float32)
        upstream = upstream_norm * gain
        inner = jnp.mean(upstream * normalized, axis=-1, keepdims=True)
        level = jnp.mean(upstream, axis=-1, keepdims=True)
        input_grad = r_ref[0, 0, here, :].astype(jnp.float32) + inverse_std * (
            upstream - level - normalized * inner
        )
        grad_ref[here, :] = input_grad.astype(jnp.bfloat16)
        sums_ref[0:1, :] += jnp.sum(upstream_norm * normalized, axis=0, keepdims=True)
        sums_ref[1:2, :] += jnp.sum(upstream_norm, axis=0, keepdims=True)
        return carry

    lax.fori_loop(0, ROWS // 128, block, 0)
    core = core_ref[0]
    lane = lax.broadcasted_iota(jnp.int32, (256, 128), 1)

    def product(i, carry):
        start = pl.multiple_of(i * 256, 256)
        here = pl.ds(start, 256)
        grads = grad_ref[:, here]
        sums = sums_ref[:, here].T
        sums = jnp.where(
            lane == SUMS % 128, sums[:, 0:1], jnp.where(lane == SUMS % 128 + 1, sums[:, 1:2], 0.0)
        )
        for half, out_ref in ((1 - core, send_ref), (core, keep_ref)):
            terms = lax.dot_general(
                grads, rows_ref[half], (((0,), (0,)), ((), ())), preferred_element_type=jnp.float32
            )
            out_ref[here, :512] = terms[:, :512].astype(out_ref.dtype)
            last = terms[:, 512:] + jnp.where(half == 0, sums, 0.0)
            out_ref[here, 512:] = last.astype(out_ref.dtype)
        return carry

    lax.fori_loop(0, D // 256, product, 0)


def products(core, slots, arr0, arr1, weight, grad_norm, grad_resid, gain):
    whole = pl.BlockSpec(memory_space=pltpu.VMEM)
    return pl.pallas_call(
        backward_kernel,
        out_shape=(
            jax.ShapeDtypeStruct((D, HALF), jnp.bfloat16),
            jax.ShapeDtypeStruct((D, HALF), jnp.float32),
        ),
        in_specs=[pl.BlockSpec(memory_space=pltpu.SMEM)] + [whole] * 7,
        out_specs=(whole, whole),
        scratch_shapes=[
            pltpu.VMEM((2, ROWS, HALF), jnp.bfloat16),
            pltpu.VMEM((ROWS, D), jnp.bfloat16),
            pltpu.VMEM((128, D), jnp.float32),
        ],
        compiler_params=pltpu.CompilerParams(vmem_limit_bytes=VMEM),
        name="norm_backward",
    )(core, slots, arr0, arr1, weight, grad_norm, grad_resid, gain)


def pieces():
    place = column_places()[0]
    runs = []
    at = 0
    while at < KIN:
        stop = at + 1
        while (
            stop < KIN
            and place[stop] == place[stop - 1] + 1
            and place[stop] % 128
            and stop % 128
        ):
            stop += 1
        runs.append((at, int(place[at]), stop - at))
        at = stop
    return runs


def finish_kernel(in_ref, out_ref, norm_ref):
    rows = in_ref.shape[1]
    lane = lax.broadcasted_iota(jnp.int32, (rows, 128), 1)
    runs = pieces()
    for tile in range(pl.cdiv(KIN, 128)):
        acc = None
        for at, src, size in runs:
            if at // 128 != tile:
                continue
            half, col = divmod(src, HALF)
            piece = in_ref[half, :, col // 128 * 128 : col // 128 * 128 + 128]
            shift = (at - src) % 128
            if shift:
                piece = pltpu.roll(piece, shift, 1)
            acc = piece if acc is None else jnp.where(lane >= at % 128, piece, acc)
        width = min(128, KIN - tile * 128)
        out_ref[:, tile * 128 : tile * 128 + width] = acc[:, :width]
    norm_ref[...] = in_ref[0, :, 512:640]


def finish(parts):
    rows = parts.shape[1]
    return pl.pallas_call(
        finish_kernel,
        out_shape=(
            jax.ShapeDtypeStruct((rows, KIN), jnp.float32),
            jax.ShapeDtypeStruct((rows, 128), jnp.float32),
        ),
        compiler_params=pltpu.CompilerParams(vmem_limit_bytes=VMEM),
        name="column_order",
    )(parts)


def shards(pixels, grad_norm, grad_resid, embed_weight, norm_gain, send_slot, recv_slot):
    core = lax.axis_index("core").astype(jnp.int32)[None]
    earlier = lax.ppermute(pixels[:, :, 3:4], "slab", [(i, i + 1) for i in range(3)])
    weight = lax.all_gather(embed_weight, "fsdp", axis=0, tiled=True)
    takes = recv_slot.reshape(2, GH, GW).transpose(0, 2, 1).reshape(1, ROWS)
    packed0 = packed_rows(takes, pixels, pixels, 0, 2)
    arrived0 = lax.all_to_all(packed0.reshape(16, CAP, HALF), ("z", "core"), 0, 0, tiled=True)
    packed1 = packed_rows(takes, earlier, pixels, 0, 1)
    arrived1 = lax.all_to_all(packed1.reshape(16, CAP, HALF), ("z", "core"), 0, 0, tiled=True)
    weight = padded_weight(weight)
    send, keep = products(
        core,
        send_slot.reshape(ROWS, 1),
        arrived0.reshape(16 * CAP, HALF),
        arrived1.reshape(16 * CAP, HALF),
        weight,
        grad_norm,
        grad_resid,
        norm_gain.reshape(1, D),
    )
    other = lax.ppermute(send, "core", [(0, 1), (1, 0)])
    pair = keep + other.astype(jnp.float32)
    spread = pair.astype(jnp.bfloat16).reshape(16, D // 16, HALF)
    plane = lax.all_to_all(spread, ("fsdp", "slab"), 0, 0, tiled=True)
    plane = jnp.sum(plane.astype(jnp.float32), axis=0)
    rows = plane.shape[0] // 8
    lines = lax.all_to_all(plane.reshape(8, rows, HALF), "z", 0, 0, tiled=True)
    line = jnp.sum(lines, axis=0, keepdims=True)
    lines = lax.all_to_all(jnp.broadcast_to(line, (8, rows, HALF)), "z", 0, 0, tiled=True)
    mine = lax.all_gather(lines.reshape(8 * rows, HALF), "slab", axis=0, tiled=True)
    both = lax.all_gather(mine, "core", axis=0)
    embed_grad, norm = finish(both)
    first = SUMS % 128
    return embed_grad, norm[:, first : first + 2].T


def solution(mesh):
    split = Mesh(mesh.devices.reshape(8, 2, 4, 4), ("z", "core", "slab", "fsdp"))
    dp = ("z", "core")
    return jax.shard_map(
        shards,
        mesh=split,
        in_specs=(
            P(dp, "fsdp", "slab", None, None, None),
            P("slab", "fsdp", dp, None),
            P("slab", "fsdp", dp, None),
            P("fsdp", None),
            P(),
            P("slab", "fsdp", dp),
            P("slab", "fsdp", dp),
        ),
        out_specs=(P("fsdp", None), P(None, "fsdp")),
        check_vma=False,
    )
```

```python
import jax
import jax.numpy as jnp
import numpy as np
from jax import lax
from jax.experimental import pallas as pl
from jax.experimental.pallas import tpu as pltpu
from jax.sharding import Mesh
from jax.sharding import PartitionSpec as P

GH = 16
GW = 16
PS = 14
COLOURS = 3
SIDE = 224
ROWS = 512
CAP = 64
PEERS = 16
D = 1280
KIN = 1176
GROUPS = 9
PARTS = COLOURS * PS
FRAME = PARTS * PS
SPLIT = FRAME // 2
HELD = 296
SECOND = 304
HALF = 640
TILES = HALF // 128
OWNED = D // 4
LINE = OWNED * TILES
QUARTER = LINE // 4
STEP = 80
PIECE = 56
SUMS = 96
VMEM = 60 * 1024 * 1024
ALL = pl.BlockSpec(memory_space=pltpu.VMEM)
SCALAR = pl.BlockSpec(memory_space=pltpu.SMEM)
PARAMS = pltpu.CompilerParams(vmem_limit_bytes=VMEM)
LANES = (((1,), (1,)), ((), ()))
SUBLANES = (((0,), (0,)), ((), ()))


def one_hot(match):
    return match.astype(jnp.float32).astype(jnp.bfloat16)


def iota(shape, dim):
    return lax.broadcasted_iota(jnp.int32, shape, dim)


def dot(a, b, dims=(((1,), (0,)), ((), ()))):
    return lax.dot_general(a, b, dims, preferred_element_type=jnp.float32)


def column_places():
    place = np.zeros((1, KIN), np.int32)
    for c in range(COLOURS):
        for t in range(2):
            part = c * PS * PS + np.arange(PS * PS)
            at = (c * 2 + t) * PS * PS
            place[0, at : at + PS * PS] = (1 - t) * HALF + part + np.where(part >= SPLIT, SECOND - SPLIT, 0)
    return place


def patch_kernel(valid_ref, slot_ref, fa_ref, fb_ref, out_ref, spread_ref, rows_ref, low_ref, high_ref):
    src = iota((SIDE, 256), 0)
    place = jnp.where(src >= GROUPS * PS, src + 2, src)
    spread = one_hot(iota((SIDE, 256), 1) == place)
    dst = iota((SIDE, SIDE), 0)
    regroup = one_hot(iota((SIDE, SIDE), 1) == (dst & 15) * PS + (dst >> 4))
    for k, ref in enumerate((fa_ref, fb_ref)):
        for c in range(COLOURS):
            frame = ref[0, 0, 0, c]
            wide = dot(frame, spread).astype(jnp.bfloat16)
            spread_ref[k, c] = dot(regroup, wide)

    @pl.when(valid_ref[0] == 0)
    def _():
        spread_ref[0] = jnp.zeros_like(spread_ref[0])

    lane = iota((GH, 128), 1)
    for k in range(2):
        for x in range(GW):
            tile = x // GROUPS * 128
            for j in range(TILES):
                acc = None
                used = min(GROUPS, PARTS - j * GROUPS)
                for a in range(used):
                    c, p = divmod(j * GROUPS + a, PS)
                    piece = spread_ref[k, c, p * GH : (p + 1) * GH, tile : tile + 128]
                    shift = PS * (a - x % GROUPS) % 128
                    if shift:
                        piece = pltpu.roll(piece, shift, 1)
                    acc = piece if acc is None else jnp.where(lane >= a * PS, piece, acc)
                acc = jnp.where(lane < used * PS, acc, 0.0)
                start = k * GH * GW + x * GH
                rows_ref[start : start + GH, j * 128 : (j + 1) * 128] = acc.astype(jnp.bfloat16)
    row = iota((SECOND, HALF), 0)
    column = iota((SECOND, HALF), 1)
    for begin, ref in ((0, low_ref), (SPLIT, high_ref)):
        value = row + begin
        gaps = sum((value >= n * GROUPS * PS).astype(jnp.int32) for n in range(1, TILES))
        pick = one_hot((column == value + 2 * gaps) & (row < SPLIT))
        ref[...] = dot(pick, rows_ref[...], LANES).astype(jnp.bfloat16)
    slots = slot_ref[...]
    kind = iota((16, ROWS), 0)
    digits = jnp.where(kind == 0, slots >> 6, jnp.where(kind == 1, slots & 63, 0))
    dst = iota((ROWS, ROWS), 0)
    order = one_hot(iota((ROWS, ROWS), 1) == (dst & 256) + ((dst & 15) << 4) + ((dst >> 4) & 15))
    digits = dot(order, digits.astype(jnp.float32).astype(jnp.bfloat16), LANES)
    slots = (digits[:, 0:1] * 64.0 + digits[:, 1:2]).astype(jnp.int32)
    side = iota((HELD, 128), 1) < CAP
    for i in range(PEERS // 4):
        pick = one_hot(iota((ROWS, 256), 1) + i * 256 == slots)
        low = dot(low_ref[...], pick)[:HELD]
        high = dot(high_ref[...], pick)[:HELD]
        for j in range(2):
            lo = low[:, j * 128 : (j + 1) * 128]
            hi = high[:, j * 128 : (j + 1) * 128]
            peer = i * 4 + j * 2
            out_ref[peer] = jnp.where(side, lo, pltpu.roll(hi, CAP, 1)).astype(jnp.bfloat16)
            out_ref[peer + 1] = jnp.where(side, pltpu.roll(lo, CAP, 1), hi).astype(jnp.bfloat16)


def packed_rows(valid, slots, first, second, first_at, second_at):
    block = (1, 1, 1, COLOURS, SIDE, SIDE)
    shape = (PEERS, HELD, 128)
    return pl.pallas_call(
        patch_kernel,
        out_shape=jax.ShapeDtypeStruct(shape, jnp.bfloat16),
        grid=(1,),
        in_specs=[
            SCALAR,
            pl.BlockSpec((1, ROWS), lambda i: (0, 0)),
            pl.BlockSpec(block, lambda i: (0, 0, first_at, 0, 0, 0)),
            pl.BlockSpec(block, lambda i: (0, 0, second_at, 0, 0, 0)),
        ],
        out_specs=pl.BlockSpec(shape, lambda i: (0, 0, 0)),
        scratch_shapes=[
            pltpu.VMEM((2, COLOURS, SIDE, 256), jnp.float32),
            pltpu.VMEM((ROWS, HALF), jnp.bfloat16),
            pltpu.VMEM((SECOND, ROWS), jnp.bfloat16),
            pltpu.VMEM((SECOND, ROWS), jnp.bfloat16),
        ],
        compiler_params=PARAMS,
        name="patch_rows",
    )(valid, slots, first, second)


def weight_kernel(place_ref, w_ref, out_ref):
    at = iota((256, KIN), 0) + pl.program_id(0) * 256
    pick = one_hot(at == place_ref[...])
    out_ref[...] = dot(pick, w_ref[...], LANES).astype(jnp.bfloat16)


def padded_weight(weight):
    return pl.pallas_call(
        weight_kernel,
        out_shape=jax.ShapeDtypeStruct((2 * HALF, D), jnp.bfloat16),
        grid=(5,),
        in_specs=[
            pl.BlockSpec((1, KIN), lambda i: (0, 0)),
            pl.BlockSpec((D, KIN), lambda i: (0, 0)),
        ],
        out_specs=pl.BlockSpec((256, D), lambda i: (i, 0)),
        compiler_params=PARAMS,
        name="weight_columns",
    )(jnp.asarray(column_places()), weight)


def taken_rows(slot_ref, arr_ref, cols_ref):
    side = iota((HELD, 128), 1) < CAP
    gap = jnp.zeros((SECOND - HELD, 128), jnp.float32)
    for j in range(PEERS // 2):
        even = arr_ref[2 * j].astype(jnp.float32)
        odd = arr_ref[2 * j + 1].astype(jnp.float32)
        low = jnp.where(side, even, pltpu.roll(odd, CAP, 1))
        high = jnp.where(side, pltpu.roll(even, CAP, 1), odd)
        at = slice(j * 128, (j + 1) * 128)
        cols_ref[0:SECOND, at] = jnp.concatenate([low, gap], axis=0).astype(jnp.bfloat16)
        cols_ref[SECOND : 2 * SECOND, at] = jnp.concatenate([high, gap], axis=0).astype(jnp.bfloat16)
    cols_ref[2 * SECOND :, :] = jnp.zeros((HALF - 2 * SECOND, PEERS * CAP), jnp.bfloat16)
    pick = one_hot(iota((ROWS, PEERS * CAP), 1) == slot_ref[...])
    return dot(pick, cols_ref[...], LANES).astype(jnp.bfloat16)


def first_kernel(slot_ref, arr_ref, w_ref, rows_ref, part_ref, cols_ref):
    rows_ref[...] = taken_rows(slot_ref, arr_ref, cols_ref)

    def block(i, carry):
        here = pl.ds(pl.multiple_of(i * 128, 128), 128)
        part_ref[here, :] = dot(rows_ref[here, :], w_ref[...])
        return carry

    lax.fori_loop(0, ROWS // 128, block, 0)


def first_half(slots, arrived, weight):
    return pl.pallas_call(
        first_kernel,
        out_shape=(
            jax.ShapeDtypeStruct((ROWS, HALF), jnp.bfloat16),
            jax.ShapeDtypeStruct((ROWS, D), jnp.float32),
        ),
        grid=(1,),
        in_specs=[
            pl.BlockSpec((ROWS, 1), lambda i: (0, 0)),
            pl.BlockSpec((PEERS, HELD, 128), lambda i: (0, 0, 0)),
            pl.BlockSpec((HALF, D), lambda i: (0, 0)),
        ],
        out_specs=(pl.BlockSpec((ROWS, HALF), lambda i: (0, 0)), pl.BlockSpec((ROWS, D), lambda i: (0, 0))),
        scratch_shapes=[pltpu.VMEM((HALF, PEERS * CAP), jnp.bfloat16)],
        compiler_params=PARAMS,
        name="first_half",
    )(slots, arrived, weight)


def second_kernel(core_ref, slot_ref, arr_ref, rows0_ref, rows1_ref, mine_ref, send_ref, cols_ref):
    rows1 = taken_rows(slot_ref, arr_ref, cols_ref)
    rows1_ref[...] = rows1

    @pl.when(core_ref[0] == 0)
    def _():
        mine_ref[...] = rows0_ref[...]
        send_ref[...] = rows1

    @pl.when(core_ref[0] != 0)
    def _():
        mine_ref[...] = rows1
        send_ref[...] = rows0_ref[...]


def second_half(core, slots, arrived, rows0):
    half = jax.ShapeDtypeStruct((ROWS, HALF), jnp.bfloat16)
    return pl.pallas_call(
        second_kernel,
        out_shape=(half, half, half),
        in_specs=[SCALAR, ALL, ALL, ALL],
        out_specs=(ALL, ALL, ALL),
        scratch_shapes=[pltpu.VMEM((HALF, PEERS * CAP), jnp.bfloat16)],
        compiler_params=PARAMS,
        name="second_half",
    )(core, slots, arrived, rows0)


def norm_kernel(rows_ref, part_ref, w_ref, g_ref, r_ref, gain_ref, grad_ref, sums_ref, embedded_ref):
    @pl.when(pl.program_id(0) == 0)
    def _():
        sums_ref[...] = jnp.zeros_like(sums_ref)

    embedded_ref[...] = part_ref[...] + dot(rows_ref[...], w_ref[...])
    gain = gain_ref[...]

    def block(i, carry):
        here = pl.ds(pl.multiple_of(i * 16, 16), 16)
        embedded = embedded_ref[here, :]
        deviation = embedded - jnp.mean(embedded, axis=-1, keepdims=True)
        variance = jnp.mean(deviation * deviation, axis=-1, keepdims=True)
        inverse_std = lax.rsqrt(variance + 1e-06)
        normalized = deviation * inverse_std
        upstream_norm = g_ref[0, 0, here, :].astype(jnp.float32)
        upstream = upstream_norm * gain
        inner = jnp.mean(upstream * normalized, axis=-1, keepdims=True)
        level = jnp.mean(upstream, axis=-1, keepdims=True)
        input_grad = r_ref[0, 0, here, :].astype(jnp.float32) + inverse_std * (
            upstream - level - normalized * inner
        )
        grad_ref[here, :] = input_grad.astype(jnp.bfloat16)
        gain_terms = upstream_norm * normalized
        sums_ref[0:8, :] += gain_terms[0:8] + gain_terms[8:16]
        sums_ref[8:16, :] += upstream_norm[0:8] + upstream_norm[8:16]
        return carry

    lax.fori_loop(0, 8, block, 0)


def norm_backward(rows, part, weight, grad_norm, grad_resid, gain):
    packed = pl.BlockSpec((1, 1, 128, D), lambda i: (0, 0, i, 0))
    return pl.pallas_call(
        norm_kernel,
        out_shape=(
            jax.ShapeDtypeStruct((ROWS, D), jnp.bfloat16),
            jax.ShapeDtypeStruct((16, D), jnp.float32),
        ),
        grid=(ROWS // 128,),
        in_specs=[
            pl.BlockSpec((128, HALF), lambda i: (i, 0)),
            pl.BlockSpec((128, D), lambda i: (i, 0)),
            pl.BlockSpec((HALF, D), lambda i: (1, 0)),
            packed,
            packed,
            pl.BlockSpec((1, D), lambda i: (0, 0)),
        ],
        out_specs=(pl.BlockSpec((128, D), lambda i: (i, 0)), pl.BlockSpec((16, D), lambda i: (0, 0))),
        scratch_shapes=[pltpu.VMEM((128, D), jnp.float32)],
        compiler_params=PARAMS,
        name="norm_backward",
    )(rows, part, weight, grad_norm, grad_resid, gain)


def product_kernel(core_ref, grad0_ref, grad1_ref, rows0_ref, rows1_ref, sums_ref, own_ref, send_ref, terms_ref):
    core, place = core_ref[0], core_ref[1]
    kind = iota((128, HALF), 0)
    lane = iota((HALF, 128), 1)
    for i in range(D // HALF):
        here = slice(i * HALF, (i + 1) * HALF)
        terms_ref[...] = dot(grad0_ref[:, here], rows0_ref[...], SUBLANES)
        terms_ref[...] += dot(grad1_ref[:, here], rows1_ref[...], SUBLANES)
        gain_sum = jnp.sum(sums_ref[0:8, here], axis=0, keepdims=True)
        bias_sum = jnp.sum(sums_ref[8:16, here], axis=0, keepdims=True)
        sums = jnp.where(kind == SUMS, gain_sum, jnp.where(kind == SUMS + 1, bias_sum, 0.0))
        terms_ref[:, HALF - 128 :] += sums.T
        for n in range(HALF // STEP):
            y, r = divmod(i * (HALF // STEP) + n, OWNED // STEP)
            for t in range(TILES):
                o = t * (OWNED // STEP) + r
                block = terms_ref[n * STEP : (n + 1) * STEP, t * 128 : (t + 1) * 128]
                to = jnp.where(core == 0, y, o // 5)
                at = jnp.where(core == 0, o * STEP, y * QUARTER + o % 5 * STEP)
                at = pl.ds(pl.multiple_of(at, 16), STEP)
                by = (to - place) & 3

                @pl.when(by == 0)
                def _():
                    own_ref[at, :] = block

                @pl.when(by != 0)
                def _():
                    send_ref[jnp.maximum(by - 1, 0), at, :] = block.astype(jnp.bfloat16)


def products(core, grad0, grad1, rows0, rows1, sums):
    return pl.pallas_call(
        product_kernel,
        out_shape=(
            jax.ShapeDtypeStruct((LINE, 128), jnp.float32),
            jax.ShapeDtypeStruct((3, LINE, 128), jnp.bfloat16),
        ),
        in_specs=[SCALAR] + [ALL] * 5,
        out_specs=(ALL, ALL),
        scratch_shapes=[pltpu.VMEM((HALF, HALF), jnp.float32)],
        compiler_params=PARAMS,
        name="products",
    )(core, grad0, grad1, rows0, rows1, sums)


def runs():
    place = column_places()[0]
    found = []
    at = 0
    while at < KIN:
        stop = at + 1
        while stop < KIN and place[stop] == place[stop - 1] + 1 and place[stop] % 128 and stop % 128:
            stop += 1
        found.append((at, int(place[at]), stop - at))
        at = stop
    return found


def finish_kernel(core_ref, mine_ref, other_ref, out_ref, norm_ref, held_ref, last_ref):
    here = core_ref[0] == 0
    for t in range(TILES):
        for r in range(OWNED // STEP):
            x, w = divmod(t * (OWNED // STEP) + r, 5)
            mine = mine_ref[x, w * STEP : (w + 1) * STEP, :]
            other = other_ref[x, w * STEP : (w + 1) * STEP, :]
            at = slice(r * STEP, (r + 1) * STEP)
            held_ref[t, at, :] = jnp.where(here, mine, other)
            held_ref[TILES + t, at, :] = jnp.where(here, other, mine)
    lane = iota((OWNED, 128), 1)
    for tile in range(pl.cdiv(KIN, 128)):
        acc = None
        for at, src, size in runs():
            if at // 128 != tile:
                continue
            piece = held_ref[src // 128]
            shift = (at - src) % 128
            if shift:
                piece = pltpu.roll(piece, shift, 1)
            acc = piece if acc is None else jnp.where(lane >= at % 128, piece, acc)
        width = min(128, KIN - tile * 128)
        out_ref[:, tile * 128 : tile * 128 + width] = acc[:, :width]
    last_ref[0:OWNED, :] = held_ref[TILES - 1] + held_ref[2 * TILES - 1]
    last_ref[OWNED:, :] = jnp.zeros((384 - OWNED, 128), jnp.float32)
    norm_ref[...] = last_ref[...].T[SUMS : SUMS + 2, :OWNED]


def finish(core, mine, other):
    return pl.pallas_call(
        finish_kernel,
        out_shape=(
            jax.ShapeDtypeStruct((OWNED, KIN), jnp.float32),
            jax.ShapeDtypeStruct((2, OWNED), jnp.float32),
        ),
        in_specs=[SCALAR, ALL, ALL],
        out_specs=(ALL, ALL),
        scratch_shapes=[
            pltpu.VMEM((2 * TILES, OWNED, 128), jnp.float32),
            pltpu.VMEM((384, 128), jnp.float32),
        ],
        compiler_params=PARAMS,
        name="column_order",
    )(core, mine, other)


def plane_index(core, x, y):
    return (core * 4 + x) * 4 + y


def plane_shift(by):
    pairs = []
    for x in range(4):
        for y in range(4):
            pairs.append((plane_index(0, x, y), plane_index(0, x, (y + by) % 4)))
            pairs.append((plane_index(1, x, y), plane_index(1, (x + by) % 4, y)))
    return pairs


def copies(array, axis, count):
    array = jnp.broadcast_to(array[None], (count,) + array.shape)
    return lax.all_to_all(array, axis, 0, 0, tiled=True)


def shards(pixels, grad_norm, grad_resid, embed_weight, norm_gain, send_slot, recv_slot):
    plane = ("core", "slab", "fsdp")
    core = lax.axis_index("core").astype(jnp.int32)
    x = lax.axis_index("slab").astype(jnp.int32)
    y = lax.axis_index("fsdp").astype(jnp.int32)
    place = jnp.stack([core, jnp.where(core == 0, y, x)])
    earlier = lax.ppermute(pixels[:, :, 3:4], "slab", [(i, (i + 1) % 4) for i in range(4)])
    weight = lax.all_gather(embed_weight, "fsdp", axis=0, tiled=True)
    takes = recv_slot.reshape(1, ROWS)
    sends = send_slot.reshape(ROWS, 1)
    packed0 = packed_rows(jnp.ones((1,), jnp.int32), takes, pixels, pixels, 0, 2)
    arrived0 = lax.all_to_all(packed0, ("z", "core"), 0, 0, tiled=True)
    packed1 = packed_rows((x > 0).astype(jnp.int32)[None], takes, earlier, pixels, 0, 1)
    arrived1 = lax.all_to_all(packed1, ("z", "core"), 0, 0, tiled=True)
    weight = padded_weight(weight)
    rows0, part = first_half(sends, arrived0, weight)
    rows1, mine, send = second_half(place, sends, arrived1, rows0)
    swap = [(0, 1), (1, 0)]
    theirs = lax.ppermute(send, "core", swap)
    grads, sums = norm_backward(rows1, part, weight, grad_norm, grad_resid, norm_gain.reshape(1, D))
    their_grads = lax.ppermute(grads, "core", swap)
    own, sent = products(place, grads, their_grads, mine, theirs, sums)
    terms = [lax.ppermute(sent[by - 1], plane, plane_shift(by)) for by in (1, 3, 2)]
    line = own + terms[0].astype(jnp.float32) + terms[1].astype(jnp.float32) + terms[2].astype(jnp.float32)
    across = [[plane_index(0, i, j) for i in range(4)] for j in range(4)]
    across += [[plane_index(1, i, j) for j in range(4)] for i in range(4)]
    quarters = lax.all_to_all(
        line.reshape(4, QUARTER, 128), plane, 0, 0, tiled=True, axis_index_groups=across
    )
    quarter = jnp.pad(jnp.sum(quarters, axis=0), ((0, 8 * PIECE - QUARTER), (0, 0)))
    pieces = lax.all_to_all(quarter.reshape(8, PIECE, 128), "z", 0, 0, tiled=True)
    quarter = copies(jnp.sum(pieces, axis=0), "z", 8).reshape(8 * PIECE, 128)
    line = copies(quarter, "slab", 4)
    return finish(place, line, lax.ppermute(line, "core", swap))


def solution(mesh):
    split = Mesh(mesh.devices.reshape(8, 2, 4, 4), ("z", "core", "slab", "fsdp"))
    dp = ("z", "core")
    return jax.shard_map(
        shards,
        mesh=split,
        in_specs=(
            P(dp, "fsdp", "slab", None, None, None),
            P("slab", "fsdp", dp, None),
            P("slab", "fsdp", dp, None),
            P("fsdp", None),
            P(),
            P("slab", "fsdp", dp),
            P("slab", "fsdp", dp),
        ),
        out_specs=(P("fsdp", None), P(None, "fsdp")),
        check_vma=False,
    )
```

```python
import jax
import jax.numpy as jnp
import numpy as np
from jax import lax
from jax.experimental import pallas as pl
from jax.experimental.pallas import tpu as pltpu
from jax.sharding import Mesh
from jax.sharding import PartitionSpec as P

GH = 16
GW = 16
PS = 14
COLOURS = 3
SIDE = 224
ROWS = 512
CAP = 64
PEERS = 16
D = 1280
KIN = 1176
GROUPS = 9
PARTS = COLOURS * PS
FRAME = PARTS * PS
HELD = 296
HALF = 640
TILES = HALF // 128
OWNED = D // 4
LINE = OWNED * TILES
QUARTER = LINE // 4
STEP = 80
PIECE = 56
BLOCK = 128
SUMS = 96
VMEM = 60 * 1024 * 1024
ALL = pl.BlockSpec(memory_space=pltpu.VMEM)
SCALAR = pl.BlockSpec(memory_space=pltpu.SMEM)
PARAMS = pltpu.CompilerParams(vmem_limit_bytes=VMEM)
LANES = (((1,), (1,)), ((), ()))
SUBLANES = (((0,), (0,)), ((), ()))


def one_hot(match):
    return match.astype(jnp.float32).astype(jnp.bfloat16)


def iota(shape, dim):
    return lax.broadcasted_iota(jnp.int32, shape, dim)


def dot(a, b, dims=(((1,), (0,)), ((), ()))):
    return lax.dot_general(a, b, dims, preferred_element_type=jnp.float32)


def column_places():
    place = np.zeros((1, KIN), np.int32)
    for c in range(COLOURS):
        for t in range(2):
            part = c * PS * PS + np.arange(PS * PS)
            at = (c * 2 + t) * PS * PS
            place[0, at : at + PS * PS] = (1 - t) * HALF + part
    return place


def patch_kernel(valid_ref, slot_ref, fa_ref, fb_ref, out_ref, spread_ref, rows_ref):
    src = iota((SIDE, 256), 0)
    place = jnp.where(src >= GROUPS * PS, src + 2, src)
    spread = one_hot(iota((SIDE, 256), 1) == place)
    for k, ref in enumerate((fa_ref, fb_ref)):
        for c in range(COLOURS):
            wide = dot(ref[0, 0, 0, c], spread)
            for h in range(2):
                spread_ref[k, c, h] = wide[:, h * 128 : (h + 1) * 128]

    @pl.when(valid_ref[0] == 0)
    def _():
        spread_ref[0] = jnp.zeros_like(spread_ref[0])

    lane = iota((GH, 128), 1)
    for k in range(2):
        for x in range(GW):
            here = slice((k * GW + x) * GH, (k * GW + x + 1) * GH)
            acc = None
            for n in range(PARTS):
                c, p = divmod(n, PS)
                piece = spread_ref[k, c, x // GROUPS, pl.ds(p, GH, stride=PS), :]
                shift = PS * (n - x % GROUPS) % 128
                if shift:
                    piece = pltpu.roll(piece, shift, 1)
                tile, at = divmod(PS * n, 128)
                acc = piece if acc is None else jnp.where(lane >= at, piece, acc)
                if n == PARTS - 1:
                    acc = jnp.where(lane < at + PS, acc, 0.0)
                if at + PS >= 128 or n == PARTS - 1:
                    rows_ref[here, tile * 128 : (tile + 1) * 128] = acc.astype(jnp.bfloat16)
                    acc = piece
    slots = slot_ref[...]
    kind = iota((16, ROWS), 0)
    digits = jnp.where(kind == 0, slots >> 6, jnp.where(kind == 1, slots & 63, 0))
    dst = iota((ROWS, ROWS), 0)
    order = one_hot(iota((ROWS, ROWS), 1) == (dst & 256) + ((dst & 15) << 4) + ((dst >> 4) & 15))
    digits = dot(order, digits.astype(jnp.float32).astype(jnp.bfloat16), LANES)
    slots = (digits[:, 0:1] * 64.0 + digits[:, 1:2]).astype(jnp.int32)
    side = iota((HELD, 128), 1) < CAP
    for i in range(PEERS // 4):
        pick = one_hot(iota((ROWS, 256), 1) + i * 256 == slots)
        both = dot(rows_ref[...], pick, SUBLANES)
        for j in range(2):
            lo = both[0:HELD, j * 128 : (j + 1) * 128]
            hi = both[HELD : 2 * HELD, j * 128 : (j + 1) * 128]
            peer = i * 4 + j * 2
            out_ref[peer] = jnp.where(side, lo, pltpu.roll(hi, CAP, 1)).astype(jnp.bfloat16)
            out_ref[peer + 1] = jnp.where(side, pltpu.roll(lo, CAP, 1), hi).astype(jnp.bfloat16)


def packed_rows(valid, slots, first, second, first_at, second_at):
    block = (1, 1, 1, COLOURS, SIDE, SIDE)
    shape = (PEERS, HELD, 128)
    return pl.pallas_call(
        patch_kernel,
        out_shape=jax.ShapeDtypeStruct(shape, jnp.bfloat16),
        grid=(1,),
        in_specs=[
            SCALAR,
            pl.BlockSpec((1, ROWS), lambda i: (0, 0)),
            pl.BlockSpec(block, lambda i: (0, 0, first_at, 0, 0, 0)),
            pl.BlockSpec(block, lambda i: (0, 0, second_at, 0, 0, 0)),
        ],
        out_specs=pl.BlockSpec(shape, lambda i: (0, 0, 0)),
        scratch_shapes=[
            pltpu.VMEM((2, COLOURS, 2, SIDE, 128), jnp.float32),
            pltpu.VMEM((ROWS, HALF), jnp.bfloat16),
        ],
        compiler_params=PARAMS,
        name="patch_rows",
    )(valid, slots, first, second)


def weight_kernel(place_ref, w_ref, out_ref):
    for i in range(2):
        pick = one_hot(iota((HALF, KIN), 0) + i * HALF == place_ref[...])
        out_ref[:, i * HALF : (i + 1) * HALF] = dot(w_ref[...], pick, LANES).astype(jnp.bfloat16)


def padded_weight(weight):
    return pl.pallas_call(
        weight_kernel,
        out_shape=jax.ShapeDtypeStruct((weight.shape[0], 2 * HALF), jnp.bfloat16),
        compiler_params=PARAMS,
        name="weight_columns",
    )(jnp.asarray(column_places()), weight)


def taken_rows(slot_ref, arr_ref, cols_ref):
    side = iota((HELD, 128), 1) < CAP
    for j in range(PEERS // 2):
        even = arr_ref[2 * j].astype(jnp.float32)
        odd = arr_ref[2 * j + 1].astype(jnp.float32)
        low = jnp.where(side, even, pltpu.roll(odd, CAP, 1))
        high = jnp.where(side, pltpu.roll(even, CAP, 1), odd)
        both = jnp.concatenate([low, high], axis=0).astype(jnp.bfloat16)
        cols_ref[: 2 * HELD, j * 128 : (j + 1) * 128] = both
    cols_ref[2 * HELD :, :] = jnp.zeros((HALF - 2 * HELD, PEERS * CAP), jnp.bfloat16)
    pick = one_hot(iota((ROWS, PEERS * CAP), 1) == slot_ref[...])
    return dot(pick, cols_ref[...], LANES).astype(jnp.bfloat16)


def first_kernel(slot_ref, arr_ref, w_ref, rows_ref, part_ref, cols_ref):
    rows_ref[...] = taken_rows(slot_ref, arr_ref, cols_ref)
    for i in range(ROWS // 128):
        here = slice(i * 128, (i + 1) * 128)
        part_ref[here, :] = dot(rows_ref[here, :], w_ref[:, :HALF], LANES)


def first_half(slots, arrived, weight):
    return pl.pallas_call(
        first_kernel,
        out_shape=(
            jax.ShapeDtypeStruct((ROWS, HALF), jnp.bfloat16),
            jax.ShapeDtypeStruct((ROWS, D), jnp.float32),
        ),
        in_specs=[ALL] * 3,
        out_specs=(ALL, ALL),
        scratch_shapes=[pltpu.VMEM((HALF, PEERS * CAP), jnp.bfloat16)],
        compiler_params=PARAMS,
        name="first_half",
    )(slots, arrived, weight)


def backward_kernel(core_ref, slot_ref, arr_ref, rows0_ref, part_ref, w_ref, g_ref, r_ref, gain_ref, grad_ref, mine_ref, send_ref, sums_ref, cols_ref, rows1_ref):
    rows1_ref[...] = taken_rows(slot_ref, arr_ref, cols_ref)

    @pl.when(core_ref[0] == 0)
    def _():
        mine_ref[...] = rows0_ref[...]
        send_ref[...] = rows1_ref[...]

    @pl.when(core_ref[0] != 0)
    def _():
        mine_ref[...] = rows1_ref[...]
        send_ref[...] = rows0_ref[...]

    gain = gain_ref[...]
    gain_sums = jnp.zeros((8, D), jnp.float32)
    bias_sums = jnp.zeros((8, D), jnp.float32)
    for i in range(ROWS // BLOCK):
        here = slice(i * BLOCK, (i + 1) * BLOCK)
        embedded = part_ref[here, :] + dot(rows1_ref[here, :], w_ref[:, HALF:], LANES)
        deviation = embedded - jnp.mean(embedded, axis=-1, keepdims=True)
        variance = jnp.mean(deviation * deviation, axis=-1, keepdims=True)
        inverse_std = lax.rsqrt(variance + 1e-06)
        normalized = deviation * inverse_std
        upstream_norm = g_ref[0, 0, here, :].astype(jnp.float32)
        upstream = upstream_norm * gain
        inner = jnp.mean(upstream * normalized, axis=-1, keepdims=True)
        level = jnp.mean(upstream, axis=-1, keepdims=True)
        input_grad = r_ref[0, 0, here, :].astype(jnp.float32) + inverse_std * (
            upstream - level - normalized * inner
        )
        grad_ref[here, :] = input_grad.astype(jnp.bfloat16)
        gain_sums += jnp.sum((upstream_norm * normalized).reshape(BLOCK // 8, 8, D), axis=0)
        bias_sums += jnp.sum(upstream_norm.reshape(BLOCK // 8, 8, D), axis=0)
    sums_ref[0:8, :] = gain_sums
    sums_ref[8:16, :] = bias_sums


def norm_backward(core, slots, arrived, rows0, part, weight, grad_norm, grad_resid, gain):
    half = jax.ShapeDtypeStruct((ROWS, HALF), jnp.bfloat16)
    return pl.pallas_call(
        backward_kernel,
        out_shape=(
            jax.ShapeDtypeStruct((ROWS, D), jnp.bfloat16),
            half,
            half,
            jax.ShapeDtypeStruct((16, D), jnp.float32),
        ),
        in_specs=[SCALAR] + [ALL] * 8,
        out_specs=(ALL,) * 4,
        scratch_shapes=[
            pltpu.VMEM((HALF, PEERS * CAP), jnp.bfloat16),
            pltpu.VMEM((ROWS, HALF), jnp.bfloat16),
        ],
        compiler_params=PARAMS,
        name="norm_backward",
    )(core, slots, arrived, rows0, part, weight, grad_norm, grad_resid, gain)


def product_kernel(core_ref, grad0_ref, grad1_ref, rows0_ref, rows1_ref, sums_ref, own_ref, out1_ref, out2_ref, out3_ref, terms_ref):
    core, place = core_ref[0], core_ref[1]
    kind = iota((128, HALF), 0)
    for i in range(D // HALF):
        here = slice(i * HALF, (i + 1) * HALF)
        terms_ref[...] = dot(grad0_ref[:, here], rows0_ref[...], SUBLANES) + dot(
            grad1_ref[:, here], rows1_ref[...], SUBLANES
        )
        gain_sum = jnp.sum(sums_ref[0:8, here], axis=0, keepdims=True)
        bias_sum = jnp.sum(sums_ref[8:16, here], axis=0, keepdims=True)
        sums = jnp.where(kind == SUMS, gain_sum, jnp.where(kind == SUMS + 1, bias_sum, 0.0))
        terms_ref[:, HALF - 128 :] += sums.T
        for n in range(HALF // STEP):
            y, r = divmod(i * (HALF // STEP) + n, OWNED // STEP)
            for t in range(TILES):
                o = t * (OWNED // STEP) + r
                block = terms_ref[n * STEP : (n + 1) * STEP, t * 128 : (t + 1) * 128]
                to = jnp.where(core == 0, y, o // 5)
                at = jnp.where(core == 0, o * STEP, y * QUARTER + o % 5 * STEP)
                at = pl.ds(pl.multiple_of(at, 16), STEP)
                by = (to - place) & 3
                for n_by, ref in enumerate((own_ref, out1_ref, out2_ref, out3_ref)):

                    @pl.when(by == n_by)
                    def _(ref=ref, at=at, block=block):
                        ref[at, :] = block.astype(ref.dtype)


def products(core, grad0, grad1, rows0, rows1, sums):
    sent = jax.ShapeDtypeStruct((LINE, 128), jnp.bfloat16)
    return pl.pallas_call(
        product_kernel,
        out_shape=(jax.ShapeDtypeStruct((LINE, 128), jnp.float32), sent, sent, sent),
        in_specs=[SCALAR] + [ALL] * 5,
        out_specs=(ALL,) * 4,
        scratch_shapes=[pltpu.VMEM((HALF, HALF), jnp.float32)],
        compiler_params=PARAMS,
        name="products",
    )(core, grad0, grad1, rows0, rows1, sums)


def runs():
    place = column_places()[0]
    found = []
    at = 0
    while at < KIN:
        stop = at + 1
        while stop < KIN and place[stop] == place[stop - 1] + 1 and place[stop] % 128 and stop % 128:
            stop += 1
        found.append((at, int(place[at]), stop - at))
        at = stop
    return found


def finish_kernel(core_ref, mine_ref, other_ref, out_ref, norm_ref, held_ref, last_ref):
    core = core_ref[0]
    for t in range(TILES):
        for r in range(OWNED // STEP):
            x, w = divmod(t * (OWNED // STEP) + r, 5)
            source = slice(x * 8 * PIECE + w * STEP, x * 8 * PIECE + (w + 1) * STEP)
            at = slice(r * STEP, (r + 1) * STEP)
            held_ref[core * TILES + t, at, :] = mine_ref[source, :]
            held_ref[(1 - core) * TILES + t, at, :] = other_ref[source, :]
    lane = iota((OWNED, 128), 1)
    for tile in range(pl.cdiv(KIN, 128)):
        acc = None
        for at, src, size in runs():
            if at // 128 != tile:
                continue
            piece = held_ref[src // 128]
            shift = (at - src) % 128
            if shift:
                piece = pltpu.roll(piece, shift, 1)
            acc = piece if acc is None else jnp.where(lane >= at % 128, piece, acc)
        width = min(128, KIN - tile * 128)
        out_ref[:, tile * 128 : tile * 128 + width] = acc[:, :width]
    last_ref[0:OWNED, :] = held_ref[TILES - 1] + held_ref[2 * TILES - 1]
    last_ref[OWNED:, :] = jnp.zeros((384 - OWNED, 128), jnp.float32)
    norm_ref[...] = last_ref[...].T[SUMS : SUMS + 2, :OWNED]


def finish(core, mine, other):
    return pl.pallas_call(
        finish_kernel,
        out_shape=(
            jax.ShapeDtypeStruct((OWNED, KIN), jnp.float32),
            jax.ShapeDtypeStruct((2, OWNED), jnp.float32),
        ),
        in_specs=[SCALAR, ALL, ALL],
        out_specs=(ALL, ALL),
        scratch_shapes=[
            pltpu.VMEM((2 * TILES, OWNED, 128), jnp.float32),
            pltpu.VMEM((384, 128), jnp.float32),
        ],
        compiler_params=PARAMS,
        name="column_order",
    )(core, mine, other)


def plane_index(core, x, y):
    return (core * 4 + x) * 4 + y


def plane_shift(by):
    pairs = []
    for x in range(4):
        for y in range(4):
            pairs.append((plane_index(0, x, y), plane_index(0, x, (y + by) % 4)))
            pairs.append((plane_index(1, x, y), plane_index(1, (x + by) % 4, y)))
    return pairs


def copies(array, axis, count):
    array = jnp.broadcast_to(array[None], (count,) + array.shape)
    return lax.all_to_all(array, axis, 0, 0, tiled=True)


def shards(pixels, grad_norm, grad_resid, embed_weight, norm_gain, send_slot, recv_slot):
    plane = ("core", "slab", "fsdp")
    core = lax.axis_index("core").astype(jnp.int32)
    x = lax.axis_index("slab").astype(jnp.int32)
    y = lax.axis_index("fsdp").astype(jnp.int32)
    place = jnp.stack([core, jnp.where(core == 0, y, x)])
    earlier = lax.ppermute(pixels[:, :, 3:4], "slab", [(i, (i + 1) % 4) for i in range(4)])
    takes = recv_slot.reshape(1, ROWS)
    sends = send_slot.reshape(ROWS, 1)
    packed0 = packed_rows(jnp.ones((1,), jnp.int32), takes, pixels, pixels, 0, 2)
    packed0, embed_weight = lax.optimization_barrier((packed0, embed_weight))
    arrived0 = lax.all_to_all(packed0, ("z", "core"), 0, 0, tiled=True)
    weight = lax.all_gather(padded_weight(embed_weight), "fsdp", axis=0, tiled=True)
    packed1 = packed_rows((x > 0).astype(jnp.int32)[None], takes, earlier, pixels, 0, 1)
    arrived1 = lax.all_to_all(packed1, ("z", "core"), 0, 0, tiled=True)
    rows0, part = first_half(sends, arrived0, weight)
    grads, mine, send, sums = norm_backward(
        place, sends, arrived1, rows0, part, weight, grad_norm, grad_resid, norm_gain.reshape(1, D)
    )
    swap = [(0, 1), (1, 0)]
    theirs = lax.ppermute(send, "core", swap)
    their_grads = lax.ppermute(grads, "core", swap)
    own, *sent = products(place, grads, their_grads, mine, theirs, sums)
    terms = [lax.ppermute(sent[by - 1], plane, plane_shift(by)) for by in (1, 3, 2)]
    line = own + terms[0].astype(jnp.float32) + terms[1].astype(jnp.float32) + terms[2].astype(jnp.float32)
    across = [[plane_index(0, i, j) for i in range(4)] for j in range(4)]
    across += [[plane_index(1, i, j) for j in range(4)] for i in range(4)]
    quarters = lax.all_to_all(
        line.reshape(4, QUARTER, 128), plane, 0, 0, tiled=True, axis_index_groups=across
    )
    quarter = jnp.pad(jnp.sum(quarters, axis=0), ((0, 8 * PIECE - QUARTER), (0, 0)))
    pieces = lax.all_to_all(quarter.reshape(8, PIECE, 128), "z", 0, 0, tiled=True)
    line = copies(jnp.sum(pieces, axis=0), ("slab", "z"), 32).reshape(32 * PIECE, 128)
    return finish(place, line, lax.ppermute(line, "core", swap))


def solution(mesh):
    split = Mesh(mesh.devices.reshape(8, 2, 4, 4), ("z", "core", "slab", "fsdp"))
    dp = ("z", "core")
    return jax.shard_map(
        shards,
        mesh=split,
        in_specs=(
            P(dp, "fsdp", "slab", None, None, None),
            P("slab", "fsdp", dp, None),
            P("slab", "fsdp", dp, None),
            P("fsdp", None),
            P(),
            P("slab", "fsdp", dp),
            P("slab", "fsdp", dp),
        ),
        out_specs=(P("fsdp", None), P(None, "fsdp")),
        check_vma=False,
    )
```

```python
import jax
import jax.numpy as jnp
import numpy as np
from jax import lax
from jax.experimental import pallas as pl
from jax.experimental.pallas import tpu as pltpu
from jax.sharding import Mesh
from jax.sharding import PartitionSpec as P

GH = 16
GW = 16
PS = 14
COLOURS = 3
SIDE = 224
ROWS = 512
CAP = 64
PEERS = 16
D = 1280
KIN = 1176
GROUPS = 9
PARTS = COLOURS * PS
FRAME = PARTS * PS
HELD = 296
HALF = 640
TILES = HALF // 128
OWNED = D // 4
LINE = OWNED * TILES
QUARTER = LINE // 4
STEP = 80
PIECE = 56
BLOCK = 128
SUMS = 96
ALL = pl.BlockSpec(memory_space=pltpu.VMEM)
SCALAR = pl.BlockSpec(memory_space=pltpu.SMEM)
PARAMS = pltpu.CompilerParams(vmem_limit_bytes=24 * 1024 * 1024)
WIDE = pltpu.CompilerParams(vmem_limit_bytes=60 * 1024 * 1024)
LANES = (((1,), (1,)), ((), ()))
SUBLANES = (((0,), (0,)), ((), ()))


def one_hot(match):
    return match.astype(jnp.float32).astype(jnp.bfloat16)


def iota(shape, dim):
    return lax.broadcasted_iota(jnp.int32, shape, dim)


def dot(a, b, dims=(((1,), (0,)), ((), ()))):
    return lax.dot_general(a, b, dims, preferred_element_type=jnp.float32)


def column_places():
    place = np.zeros((1, KIN), np.int32)
    for c in range(COLOURS):
        for t in range(2):
            part = c * PS * PS + np.arange(PS * PS)
            at = (c * 2 + t) * PS * PS
            place[0, at : at + PS * PS] = (1 - t) * HALF + part
    return place


def patch_kernel(valid_ref, slot_ref, fa_ref, fb_ref, out_ref, spread_ref, rows_ref):
    src = iota((SIDE, 256), 0)
    place = jnp.where(src >= GROUPS * PS, src + 2, src)
    spread = one_hot(iota((SIDE, 256), 1) == place)
    for k, ref in enumerate((fa_ref, fb_ref)):
        for c in range(COLOURS):
            wide = dot(ref[0, 0, 0, c], spread)
            for h in range(2):
                spread_ref[k, c, h] = wide[:, h * 128 : (h + 1) * 128]

    @pl.when(valid_ref[0] == 0)
    def _():
        spread_ref[0] = jnp.zeros_like(spread_ref[0])

    lane = iota((GH, 128), 1)
    for k in range(2):
        for x in range(GW):
            here = slice((k * GW + x) * GH, (k * GW + x + 1) * GH)
            acc = None
            for n in range(PARTS):
                c, p = divmod(n, PS)
                piece = spread_ref[k, c, x // GROUPS, pl.ds(p, GH, stride=PS), :]
                shift = PS * (n - x % GROUPS) % 128
                if shift:
                    piece = pltpu.roll(piece, shift, 1)
                tile, at = divmod(PS * n, 128)
                acc = piece if acc is None else jnp.where(lane >= at, piece, acc)
                if n == PARTS - 1:
                    acc = jnp.where(lane < at + PS, acc, 0.0)
                if at + PS >= 128 or n == PARTS - 1:
                    rows_ref[here, tile * 128 : (tile + 1) * 128] = acc.astype(jnp.bfloat16)
                    acc = piece
    slots = slot_ref[...]
    kind = iota((16, ROWS), 0)
    digits = jnp.where(kind == 0, slots >> 6, jnp.where(kind == 1, slots & 63, 0))
    dst = iota((ROWS, ROWS), 0)
    order = one_hot(iota((ROWS, ROWS), 1) == (dst & 256) + ((dst & 15) << 4) + ((dst >> 4) & 15))
    digits = dot(order, digits.astype(jnp.float32).astype(jnp.bfloat16), LANES)
    slots = (digits[:, 0:1] * 64.0 + digits[:, 1:2]).astype(jnp.int32)
    side = iota((HELD, 128), 1) < CAP
    for i in range(PEERS // 4):
        pick = one_hot(iota((ROWS, 256), 1) + i * 256 == slots)
        both = dot(rows_ref[...], pick, SUBLANES)
        for j in range(2):
            lo = both[0:HELD, j * 128 : (j + 1) * 128]
            hi = both[HELD : 2 * HELD, j * 128 : (j + 1) * 128]
            peer = i * 4 + j * 2
            out_ref[peer] = jnp.where(side, lo, pltpu.roll(hi, CAP, 1)).astype(jnp.bfloat16)
            out_ref[peer + 1] = jnp.where(side, pltpu.roll(lo, CAP, 1), hi).astype(jnp.bfloat16)


def packed_rows(valid, slots, first, second, first_at, second_at):
    block = (1, 1, 1, COLOURS, SIDE, SIDE)
    shape = (PEERS, HELD, 128)
    return pl.pallas_call(
        patch_kernel,
        out_shape=jax.ShapeDtypeStruct(shape, jnp.bfloat16),
        grid=(1,),
        in_specs=[
            SCALAR,
            pl.BlockSpec((1, ROWS), lambda i: (0, 0)),
            pl.BlockSpec(block, lambda i: (0, 0, first_at, 0, 0, 0)),
            pl.BlockSpec(block, lambda i: (0, 0, second_at, 0, 0, 0)),
        ],
        out_specs=pl.BlockSpec(shape, lambda i: (0, 0, 0)),
        scratch_shapes=[
            pltpu.VMEM((2, COLOURS, 2, SIDE, 128), jnp.float32),
            pltpu.VMEM((ROWS, HALF), jnp.bfloat16),
        ],
        compiler_params=WIDE,
        name="patch_rows",
    )(valid, slots, first, second)


def weight_kernel(place_ref, column_ref, own_ref, *refs):
    *parts, out_ref, held_ref = refs
    core, y = place_ref[0], place_ref[2]
    part = OWNED // 2
    held_ref[pl.ds(pl.multiple_of(y * OWNED, 16), OWNED), :] = own_ref[...]
    for n, ref in enumerate(parts):
        side, by = divmod(n, 3)
        row = ((y - by - 1) & 3) * OWNED + (core if side == 0 else 1 - core) * part
        held_ref[pl.ds(pl.multiple_of(row, 16), part), :] = ref[...]
    for i in range(2):
        pick = one_hot(iota((HALF, KIN), 0) + i * HALF == column_ref[...])
        out_ref[:, i * HALF : (i + 1) * HALF] = dot(held_ref[...], pick, LANES).astype(jnp.bfloat16)


def padded_weight(place, own, parts):
    return pl.pallas_call(
        weight_kernel,
        out_shape=jax.ShapeDtypeStruct((D, 2 * HALF), jnp.bfloat16),
        in_specs=[SCALAR] + [ALL] * 8,
        out_specs=ALL,
        scratch_shapes=[pltpu.VMEM((D, KIN), jnp.bfloat16)],
        compiler_params=WIDE,
        name="weight_columns",
    )(place, jnp.asarray(column_places()), own, *parts)


def taken_rows(slot_ref, arr_ref, cols_ref):
    side = iota((HELD, 128), 1) < CAP
    for j in range(PEERS // 2):
        even = arr_ref[2 * j].astype(jnp.float32)
        odd = arr_ref[2 * j + 1].astype(jnp.float32)
        low = jnp.where(side, even, pltpu.roll(odd, CAP, 1))
        high = jnp.where(side, pltpu.roll(even, CAP, 1), odd)
        both = jnp.concatenate([low, high], axis=0).astype(jnp.bfloat16)
        cols_ref[: 2 * HELD, j * 128 : (j + 1) * 128] = both
    cols_ref[2 * HELD :, :] = jnp.zeros((HALF - 2 * HELD, PEERS * CAP), jnp.bfloat16)
    pick = one_hot(iota((ROWS, PEERS * CAP), 1) == slot_ref[...])
    return dot(pick, cols_ref[...], LANES).astype(jnp.bfloat16)


def first_kernel(slot_ref, arr_ref, w_ref, rows_ref, part_ref, cols_ref):
    rows_ref[...] = taken_rows(slot_ref, arr_ref, cols_ref)
    for i in range(ROWS // 128):
        here = slice(i * 128, (i + 1) * 128)
        part_ref[here, :] = dot(rows_ref[here, :], w_ref[:, :HALF], LANES)


def first_half(slots, arrived, weight):
    return pl.pallas_call(
        first_kernel,
        out_shape=(
            jax.ShapeDtypeStruct((ROWS, HALF), jnp.bfloat16),
            jax.ShapeDtypeStruct((ROWS, D), jnp.float32),
        ),
        in_specs=[ALL] * 3,
        out_specs=(ALL, ALL),
        scratch_shapes=[pltpu.VMEM((HALF, PEERS * CAP), jnp.bfloat16)],
        compiler_params=WIDE,
        name="first_half",
    )(slots, arrived, weight)


def backward_kernel(core_ref, slot_ref, arr_ref, rows0_ref, part_ref, w_ref, g_ref, r_ref, gain_ref, grad_ref, mine_ref, send_ref, sums_ref, cols_ref, rows1_ref):
    step = pl.program_id(0)

    @pl.when(step == 0)
    def _():
        rows1_ref[...] = taken_rows(slot_ref, arr_ref, cols_ref)
        sums_ref[...] = jnp.zeros_like(sums_ref)

    here = pl.ds(pl.multiple_of(step * BLOCK, BLOCK), BLOCK)

    @pl.when(core_ref[0] == 0)
    def _():
        mine_ref[...] = rows0_ref[...]
        send_ref[...] = rows1_ref[here, :]

    @pl.when(core_ref[0] != 0)
    def _():
        mine_ref[...] = rows1_ref[here, :]
        send_ref[...] = rows0_ref[...]

    embedded = part_ref[...] + dot(rows1_ref[here, :], w_ref[...], LANES)
    deviation = embedded - jnp.mean(embedded, axis=-1, keepdims=True)
    variance = jnp.mean(deviation * deviation, axis=-1, keepdims=True)
    inverse_std = lax.rsqrt(variance + 1e-06)
    normalized = deviation * inverse_std
    upstream_norm = g_ref[0, 0].astype(jnp.float32)
    upstream = upstream_norm * gain_ref[...]
    inner = jnp.mean(upstream * normalized, axis=-1, keepdims=True)
    level = jnp.mean(upstream, axis=-1, keepdims=True)
    input_grad = r_ref[0, 0].astype(jnp.float32) + inverse_std * (upstream - level - normalized * inner)
    grad_ref[...] = input_grad.astype(jnp.bfloat16)
    sums_ref[0:8, :] += jnp.sum((upstream_norm * normalized).reshape(BLOCK // 8, 8, D), axis=0)
    sums_ref[8:16, :] += jnp.sum(upstream_norm.reshape(BLOCK // 8, 8, D), axis=0)


def norm_backward(core, slots, arrived, rows0, part, weight, grad_norm, grad_resid, gain):
    half = jax.ShapeDtypeStruct((ROWS, HALF), jnp.bfloat16)
    packed = pl.BlockSpec((1, 1, BLOCK, D), lambda i: (0, 0, i, 0))
    rows = pl.BlockSpec((BLOCK, D), lambda i: (i, 0))
    halves = pl.BlockSpec((BLOCK, HALF), lambda i: (i, 0))
    return pl.pallas_call(
        backward_kernel,
        out_shape=(
            jax.ShapeDtypeStruct((ROWS, D), jnp.bfloat16),
            half,
            half,
            jax.ShapeDtypeStruct((16, D), jnp.float32),
        ),
        grid=(ROWS // BLOCK,),
        in_specs=[
            SCALAR,
            pl.BlockSpec((ROWS, 1), lambda i: (0, 0)),
            pl.BlockSpec((PEERS, HELD, 128), lambda i: (0, 0, 0)),
            halves,
            rows,
            pl.BlockSpec((D, HALF), lambda i: (0, 1)),
            packed,
            packed,
            pl.BlockSpec((1, D), lambda i: (0, 0)),
        ],
        out_specs=(rows, halves, halves, pl.BlockSpec((16, D), lambda i: (0, 0))),
        scratch_shapes=[
            pltpu.VMEM((HALF, PEERS * CAP), jnp.bfloat16),
            pltpu.VMEM((ROWS, HALF), jnp.bfloat16),
        ],
        compiler_params=WIDE,
        name="norm_backward",
    )(core, slots, arrived, rows0, part, weight, grad_norm, grad_resid, gain)


def product_kernel(core_ref, grad0_ref, grad1_ref, rows0_ref, rows1_ref, sums_ref, own_ref, out1_ref, out2_ref, out3_ref, terms_ref, order_ref):
    core, place = core_ref[0], core_ref[1]
    kind = iota((128, HALF), 0)
    for i in range(D // HALF):
        here = slice(i * HALF, (i + 1) * HALF)
        terms_ref[...] = dot(grad0_ref[:, here], rows0_ref[...], SUBLANES) + dot(
            grad1_ref[:, here], rows1_ref[...], SUBLANES
        )
        gain_sum = jnp.sum(sums_ref[0:8, here], axis=0, keepdims=True)
        bias_sum = jnp.sum(sums_ref[8:16, here], axis=0, keepdims=True)
        sums = jnp.where(kind == SUMS, gain_sum, jnp.where(kind == SUMS + 1, bias_sum, 0.0))
        terms_ref[:, HALF - 128 :] += sums.T
        for n in range(HALF // STEP):
            y, r = divmod(i * (HALF // STEP) + n, OWNED // STEP)
            for t in range(TILES):
                o = t * (OWNED // STEP) + r
                block = terms_ref[n * STEP : (n + 1) * STEP, t * 128 : (t + 1) * 128]
                to = jnp.where(core == 0, y, o // 5)
                at = jnp.where(core == 0, o * STEP, y * QUARTER + o % 5 * STEP)
                at = pl.ds(pl.multiple_of(at, 16), STEP)
                order_ref[(to - place) & 3, at, :] = block
    own_ref[...] = order_ref[0]
    for by, ref in enumerate((out1_ref, out2_ref, out3_ref)):
        ref[...] = order_ref[by + 1].astype(jnp.bfloat16)


def products(core, grad0, grad1, rows0, rows1, sums):
    sent = jax.ShapeDtypeStruct((LINE, 128), jnp.bfloat16)
    return pl.pallas_call(
        product_kernel,
        out_shape=(jax.ShapeDtypeStruct((LINE, 128), jnp.float32), sent, sent, sent),
        in_specs=[SCALAR] + [ALL] * 5,
        out_specs=(ALL,) * 4,
        scratch_shapes=[
            pltpu.VMEM((HALF, HALF), jnp.float32),
            pltpu.VMEM((4, LINE, 128), jnp.float32),
        ],
        compiler_params=PARAMS,
        name="products",
    )(core, grad0, grad1, rows0, rows1, sums)


def runs():
    place = column_places()[0]
    found = []
    at = 0
    while at < KIN:
        stop = at + 1
        while stop < KIN and place[stop] == place[stop - 1] + 1 and place[stop] % 128 and stop % 128:
            stop += 1
        found.append((at, int(place[at]), stop - at))
        at = stop
    return found


def finish_kernel(core_ref, mine_ref, other_ref, out_ref, norm_ref, held_ref, last_ref):
    core = core_ref[0]
    for t in range(TILES):
        held_ref[core * TILES + t] = mine_ref[t * OWNED : (t + 1) * OWNED, :]
        held_ref[(1 - core) * TILES + t] = other_ref[t * OWNED : (t + 1) * OWNED, :]
    lane = iota((OWNED, 128), 1)
    for tile in range(pl.cdiv(KIN, 128)):
        acc = None
        for at, src, size in runs():
            if at // 128 != tile:
                continue
            piece = held_ref[src // 128]
            shift = (at - src) % 128
            if shift:
                piece = pltpu.roll(piece, shift, 1)
            acc = piece if acc is None else jnp.where(lane >= at % 128, piece, acc)
        width = min(128, KIN - tile * 128)
        out_ref[:, tile * 128 : tile * 128 + width] = acc[:, :width]
    last_ref[0:OWNED, :] = held_ref[TILES - 1] + held_ref[2 * TILES - 1]
    last_ref[OWNED:, :] = jnp.zeros((384 - OWNED, 128), jnp.float32)
    norm_ref[...] = last_ref[...].T[SUMS : SUMS + 2, :OWNED]


def finish(core, mine, other):
    return pl.pallas_call(
        finish_kernel,
        out_shape=(
            jax.ShapeDtypeStruct((OWNED, KIN), jnp.float32),
            jax.ShapeDtypeStruct((2, OWNED), jnp.float32),
        ),
        in_specs=[SCALAR, ALL, ALL],
        out_specs=(ALL, ALL),
        scratch_shapes=[
            pltpu.VMEM((2 * TILES, OWNED, 128), jnp.float32),
            pltpu.VMEM((384, 128), jnp.float32),
        ],
        compiler_params=PARAMS,
        name="column_order",
    )(core, mine, other)


def plane_index(core, x, y):
    return (core * 4 + x) * 4 + y


def plane_shift(by):
    pairs = []
    for x in range(4):
        for y in range(4):
            pairs.append((plane_index(0, x, y), plane_index(0, x, (y + by) % 4)))
            pairs.append((plane_index(1, x, y), plane_index(1, (x + by) % 4, y)))
    return pairs


def copies(array, axis, count):
    array = jnp.broadcast_to(array[None], (count,) + array.shape)
    return lax.all_to_all(array, axis, 0, 0, tiled=True)


def shards(pixels, grad_norm, grad_resid, embed_weight, norm_gain, send_slot, recv_slot):
    plane = ("core", "slab", "fsdp")
    core = lax.axis_index("core").astype(jnp.int32)
    x = lax.axis_index("slab").astype(jnp.int32)
    y = lax.axis_index("fsdp").astype(jnp.int32)
    place = jnp.stack([core, jnp.where(core == 0, y, x), y])
    earlier = lax.ppermute(pixels[:, :, 3:4], "slab", [(i, (i + 1) % 4) for i in range(4)])
    takes = recv_slot.reshape(1, ROWS)
    sends = send_slot.reshape(ROWS, 1)
    packed0 = packed_rows(jnp.ones((1,), jnp.int32), takes, pixels, pixels, 0, 2)
    packed0, shard = lax.optimization_barrier((packed0, embed_weight))
    arrived0 = lax.all_to_all(packed0, ("z", "core"), 0, 0, tiled=True)
    swap = [(0, 1), (1, 0)]
    part = lax.dynamic_slice_in_dim(shard, core * (OWNED // 2), OWNED // 2, 0)
    parts = [lax.ppermute(part, "fsdp", [(i, (i + by) % 4) for i in range(4)]) for by in (1, 2, 3)]
    earlier, *parts = lax.optimization_barrier((earlier, *parts))
    packed1 = packed_rows((x > 0).astype(jnp.int32)[None], takes, earlier, pixels, 0, 1)
    arrived1 = lax.all_to_all(packed1, ("z", "core"), 0, 0, tiled=True)
    parts += [lax.ppermute(part, "core", swap) for part in parts]
    weight = padded_weight(place, embed_weight, parts)
    rows0, part = first_half(sends, arrived0, weight)
    grads, mine, send, sums = norm_backward(
        place, sends, arrived1, rows0, part, weight, grad_norm, grad_resid, norm_gain.reshape(1, D)
    )
    theirs = lax.ppermute(send, "core", swap)
    their_grads = lax.ppermute(grads, "core", swap)
    own, *sent = products(place, grads, their_grads, mine, theirs, sums)
    terms = [lax.ppermute(sent[by - 1], plane, plane_shift(by)) for by in (1, 3, 2)]
    line = own + terms[0].astype(jnp.float32) + terms[1].astype(jnp.float32) + terms[2].astype(jnp.float32)
    across = [[plane_index(0, i, j) for i in range(4)] for j in range(4)]
    across += [[plane_index(1, i, j) for j in range(4)] for i in range(4)]
    quarters = lax.all_to_all(
        line.reshape(4, QUARTER, 128), plane, 0, 0, tiled=True, axis_index_groups=across
    )
    quarter = jnp.pad(jnp.sum(quarters, axis=0), ((0, 8 * PIECE - QUARTER), (0, 0)))
    pieces = lax.all_to_all(quarter.reshape(8, PIECE, 128), "z", 0, 0, tiled=True)
    quarter = copies(jnp.sum(pieces, axis=0), "z", 8).reshape(8 * PIECE, 128)[:QUARTER]
    line = copies(quarter, "slab", 4).reshape(LINE, 128)
    return finish(place, line, lax.ppermute(line, "core", swap))


def solution(mesh):
    split = Mesh(mesh.devices.reshape(8, 2, 4, 4), ("z", "core", "slab", "fsdp"))
    dp = ("z", "core")
    return jax.shard_map(
        shards,
        mesh=split,
        in_specs=(
            P(dp, "fsdp", "slab", None, None, None),
            P("slab", "fsdp", dp, None),
            P("slab", "fsdp", dp, None),
            P("fsdp", None),
            P(),
            P("slab", "fsdp", dp),
            P("slab", "fsdp", dp),
        ),
        out_specs=(P("fsdp", None), P(None, "fsdp")),
        check_vma=False,
    )
```

```python
import jax
import jax.numpy as jnp
import numpy as np
from jax import lax
from jax.experimental import pallas as pl
from jax.experimental.pallas import tpu as pltpu
from jax.sharding import Mesh
from jax.sharding import PartitionSpec as P

GH = 16
GW = 16
PS = 14
COLOURS = 3
SIDE = 224
ROWS = 512
CAP = 64
PEERS = 16
D = 1280
KIN = 1176
GROUPS = 9
PARTS = COLOURS * PS
FRAME = PARTS * PS
HELD = 296
HALF = 640
TILES = HALF // 128
OWNED = D // 4
LINE = OWNED * TILES
QUARTER = LINE // 4
STEP = 80
PIECE = 56
BLOCK = 128
SUMS = 96
ALL = pl.BlockSpec(memory_space=pltpu.VMEM)
FAR = pl.BlockSpec(memory_space=pltpu.HBM)
SCALAR = pl.BlockSpec(memory_space=pltpu.SMEM)
PARAMS = pltpu.CompilerParams(vmem_limit_bytes=24 * 1024 * 1024)
NORM = pltpu.CompilerParams(vmem_limit_bytes=49 * 1024 * 1024)
WIDE = pltpu.CompilerParams(vmem_limit_bytes=60 * 1024 * 1024)
LANES = (((1,), (1,)), ((), ()))
SUBLANES = (((0,), (0,)), ((), ()))


def one_hot(match):
    return match.astype(jnp.float32).astype(jnp.bfloat16)


def iota(shape, dim):
    return lax.broadcasted_iota(jnp.int32, shape, dim)


def dot(a, b, dims=(((1,), (0,)), ((), ()))):
    return lax.dot_general(a, b, dims, preferred_element_type=jnp.float32)


def column_places():
    place = np.zeros((1, KIN), np.int32)
    for c in range(COLOURS):
        for t in range(2):
            part = c * PS * PS + np.arange(PS * PS)
            at = (c * 2 + t) * PS * PS
            place[0, at : at + PS * PS] = (1 - t) * HALF + part
    return place


def patch_kernel(valid_ref, slot_ref, fa_ref, fb_ref, out_ref, spread_ref, rows_ref):
    src = iota((SIDE, 256), 0)
    place = jnp.where(src >= GROUPS * PS, src + 2, src)
    spread = one_hot(iota((SIDE, 256), 1) == place)
    for k, ref in enumerate((fa_ref, fb_ref)):
        for c in range(COLOURS):
            wide = dot(ref[0, 0, 0, c], spread)
            for h in range(2):
                spread_ref[k, c, h] = wide[:, h * 128 : (h + 1) * 128]

    @pl.when(valid_ref[0] == 0)
    def _():
        spread_ref[0] = jnp.zeros_like(spread_ref[0])

    lane = iota((GH, 128), 1)
    for k in range(2):
        for x in range(GW):
            here = slice((k * GW + x) * GH, (k * GW + x + 1) * GH)
            acc = None
            for n in range(PARTS):
                c, p = divmod(n, PS)
                piece = spread_ref[k, c, x // GROUPS, pl.ds(p, GH, stride=PS), :]
                shift = PS * (n - x % GROUPS) % 128
                if shift:
                    piece = pltpu.roll(piece, shift, 1)
                tile, at = divmod(PS * n, 128)
                acc = piece if acc is None else jnp.where(lane >= at, piece, acc)
                if n == PARTS - 1:
                    acc = jnp.where(lane < at + PS, acc, 0.0)
                if at + PS >= 128 or n == PARTS - 1:
                    rows_ref[here, tile * 128 : (tile + 1) * 128] = acc.astype(jnp.bfloat16)
                    acc = piece
    slots = slot_ref[...]
    kind = iota((16, ROWS), 0)
    digits = jnp.where(kind == 0, slots >> 6, jnp.where(kind == 1, slots & 63, 0))
    dst = iota((ROWS, ROWS), 0)
    order = one_hot(iota((ROWS, ROWS), 1) == (dst & 256) + ((dst & 15) << 4) + ((dst >> 4) & 15))
    digits = dot(order, digits.astype(jnp.float32).astype(jnp.bfloat16), LANES)
    slots = (digits[:, 0:1] * 64.0 + digits[:, 1:2]).astype(jnp.int32)
    side = iota((HELD, 128), 1) < CAP
    for i in range(PEERS // 4):
        pick = one_hot(iota((ROWS, 256), 1) + i * 256 == slots)
        both = dot(rows_ref[...], pick, SUBLANES)
        for j in range(2):
            lo = both[0:HELD, j * 128 : (j + 1) * 128]
            hi = both[HELD : 2 * HELD, j * 128 : (j + 1) * 128]
            peer = i * 4 + j * 2
            out_ref[peer] = jnp.where(side, lo, pltpu.roll(hi, CAP, 1)).astype(jnp.bfloat16)
            out_ref[peer + 1] = jnp.where(side, pltpu.roll(lo, CAP, 1), hi).astype(jnp.bfloat16)


def packed_rows(valid, slots, first, second, first_at, second_at):
    block = (1, 1, 1, COLOURS, SIDE, SIDE)
    shape = (PEERS, HELD, 128)
    return pl.pallas_call(
        patch_kernel,
        out_shape=jax.ShapeDtypeStruct(shape, jnp.bfloat16),
        grid=(1,),
        in_specs=[
            SCALAR,
            pl.BlockSpec((1, ROWS), lambda i: (0, 0)),
            pl.BlockSpec(block, lambda i: (0, 0, first_at, 0, 0, 0)),
            pl.BlockSpec(block, lambda i: (0, 0, second_at, 0, 0, 0)),
        ],
        out_specs=pl.BlockSpec(shape, lambda i: (0, 0, 0)),
        scratch_shapes=[
            pltpu.VMEM((2, COLOURS, 2, SIDE, 128), jnp.float32),
            pltpu.VMEM((ROWS, HALF), jnp.bfloat16),
        ],
        compiler_params=WIDE,
        name="patch_rows",
    )(valid, slots, first, second)


def weight_kernel(place_ref, column_ref, own_ref, *refs):
    *parts, out_ref, held_ref = refs
    core, y = place_ref[0], place_ref[2]
    part = OWNED // 2
    held_ref[pl.ds(pl.multiple_of(y * OWNED, 16), OWNED), :] = own_ref[...]
    for n, ref in enumerate(parts):
        side, by = divmod(n, 3)
        row = ((y - by - 1) & 3) * OWNED + (core if side == 0 else 1 - core) * part
        held_ref[pl.ds(pl.multiple_of(row, 16), part), :] = ref[...]
    for i in range(2):
        pick = one_hot(iota((HALF, KIN), 0) + i * HALF == column_ref[...])
        out_ref[:, i * HALF : (i + 1) * HALF] = dot(held_ref[...], pick, LANES).astype(jnp.bfloat16)


def padded_weight(place, own, parts):
    return pl.pallas_call(
        weight_kernel,
        out_shape=jax.ShapeDtypeStruct((D, 2 * HALF), jnp.bfloat16),
        in_specs=[SCALAR] + [ALL] * 8,
        out_specs=ALL,
        scratch_shapes=[pltpu.VMEM((D, KIN), jnp.bfloat16)],
        compiler_params=WIDE,
        name="weight_columns",
    )(place, jnp.asarray(column_places()), own, *parts)


def taken_rows(slot_ref, arr_ref, cols_ref):
    side = iota((HELD, 128), 1) < CAP
    for j in range(PEERS // 2):
        even = arr_ref[2 * j].astype(jnp.float32)
        odd = arr_ref[2 * j + 1].astype(jnp.float32)
        low = jnp.where(side, even, pltpu.roll(odd, CAP, 1))
        high = jnp.where(side, pltpu.roll(even, CAP, 1), odd)
        both = jnp.concatenate([low, high], axis=0).astype(jnp.bfloat16)
        cols_ref[: 2 * HELD, j * 128 : (j + 1) * 128] = both
    cols_ref[2 * HELD :, :] = jnp.zeros((HALF - 2 * HELD, PEERS * CAP), jnp.bfloat16)
    pick = one_hot(iota((ROWS, PEERS * CAP), 1) == slot_ref[...])
    return dot(pick, cols_ref[...], LANES).astype(jnp.bfloat16)


def first_kernel(slot_ref, arr_ref, w_ref, part_ref, cols_ref, rows_ref):
    rows_ref[...] = taken_rows(slot_ref, arr_ref, cols_ref)
    for i in range(ROWS // 128):
        here = slice(i * 128, (i + 1) * 128)
        part_ref[here, :D] = dot(rows_ref[here, :], w_ref[:, :HALF], LANES)
        part_ref[here, D:] = rows_ref[here, :].astype(jnp.float32)


def first_half(slots, arrived, weight):
    return pl.pallas_call(
        first_kernel,
        out_shape=jax.ShapeDtypeStruct((ROWS, D + HALF), jnp.float32),
        in_specs=[ALL] * 3,
        out_specs=ALL,
        scratch_shapes=[
            pltpu.VMEM((HALF, PEERS * CAP), jnp.bfloat16),
            pltpu.VMEM((ROWS, HALF), jnp.bfloat16),
        ],
        compiler_params=WIDE,
        name="first_half",
    )(slots, arrived, weight)


def backward_kernel(core_ref, slot_ref, arr_ref, part_far, w_far, g_far, r_far, gain_ref, grad_ref, mine_ref, send_ref, sums_ref, cols_ref, rows1_ref, part_ref, w_ref, g_ref, r_ref, sems):
    reads = [
        pltpu.make_async_copy(w_far.at[:, HALF:], w_ref, sems.at[0]),
        pltpu.make_async_copy(part_far, part_ref, sems.at[1]),
        pltpu.make_async_copy(g_far.at[0, 0], g_ref, sems.at[2]),
        pltpu.make_async_copy(r_far.at[0, 0], r_ref, sems.at[3]),
    ]
    for read in reads:
        read.start()
    rows1_ref[...] = taken_rows(slot_ref, arr_ref, cols_ref)
    for read in reads:
        read.wait()

    @pl.when(core_ref[0] == 0)
    def _():
        mine_ref[...] = part_ref[:, D:].astype(jnp.bfloat16)
        send_ref[...] = rows1_ref[...]

    @pl.when(core_ref[0] != 0)
    def _():
        mine_ref[...] = rows1_ref[...]
        send_ref[...] = part_ref[:, D:].astype(jnp.bfloat16)

    gain = gain_ref[...]
    gain_sums = jnp.zeros((8, D), jnp.float32)
    bias_sums = jnp.zeros((8, D), jnp.float32)
    for i in range(ROWS // BLOCK):
        here = slice(i * BLOCK, (i + 1) * BLOCK)
        embedded = part_ref[here, :D] + dot(rows1_ref[here, :], w_ref[...], LANES)
        deviation = embedded - jnp.mean(embedded, axis=-1, keepdims=True)
        variance = jnp.mean(deviation * deviation, axis=-1, keepdims=True)
        inverse_std = lax.rsqrt(variance + 1e-06)
        normalized = deviation * inverse_std
        upstream_norm = g_ref[here, :].astype(jnp.float32)
        upstream = upstream_norm * gain
        inner = jnp.mean(upstream * normalized, axis=-1, keepdims=True)
        level = jnp.mean(upstream, axis=-1, keepdims=True)
        input_grad = r_ref[here, :].astype(jnp.float32) + inverse_std * (
            upstream - level - normalized * inner
        )
        grad_ref[here, :] = input_grad.astype(jnp.bfloat16)
        gain_sums += jnp.sum((upstream_norm * normalized).reshape(BLOCK // 8, 8, D), axis=0)
        bias_sums += jnp.sum(upstream_norm.reshape(BLOCK // 8, 8, D), axis=0)
    sums_ref[0:8, :] = gain_sums
    sums_ref[8:16, :] = bias_sums


def norm_backward(core, slots, arrived, part, weight, grad_norm, grad_resid, gain):
    half = jax.ShapeDtypeStruct((ROWS, HALF), jnp.bfloat16)
    return pl.pallas_call(
        backward_kernel,
        out_shape=(
            jax.ShapeDtypeStruct((ROWS, D), jnp.bfloat16),
            half,
            half,
            jax.ShapeDtypeStruct((16, D), jnp.float32),
        ),
        in_specs=[SCALAR, ALL, ALL, FAR, FAR, FAR, FAR, ALL],
        out_specs=(ALL,) * 4,
        scratch_shapes=[
            pltpu.VMEM((HALF, PEERS * CAP), jnp.bfloat16),
            pltpu.VMEM((ROWS, HALF), jnp.bfloat16),
            pltpu.VMEM((ROWS, D + HALF), jnp.float32),
            pltpu.VMEM((D, HALF), jnp.bfloat16),
            pltpu.VMEM((ROWS, D), jnp.bfloat16),
            pltpu.VMEM((ROWS, D), jnp.bfloat16),
            pltpu.SemaphoreType.DMA((4,)),
        ],
        compiler_params=NORM,
        name="norm_backward",
    )(core, slots, arrived, part, weight, grad_norm, grad_resid, gain)


def product_kernel(core_ref, grad0_ref, grad1_ref, rows0_ref, rows1_ref, sums_ref, own_ref, out1_ref, out2_ref, out3_ref, terms_ref, order_ref):
    core, place = core_ref[0], core_ref[1]
    kind = iota((128, HALF), 0)
    for i in range(D // HALF):
        here = slice(i * HALF, (i + 1) * HALF)
        terms_ref[...] = dot(grad0_ref[:, here], rows0_ref[...], SUBLANES) + dot(
            grad1_ref[:, here], rows1_ref[...], SUBLANES
        )
        gain_sum = jnp.sum(sums_ref[0:8, here], axis=0, keepdims=True)
        bias_sum = jnp.sum(sums_ref[8:16, here], axis=0, keepdims=True)
        sums = jnp.where(kind == SUMS, gain_sum, jnp.where(kind == SUMS + 1, bias_sum, 0.0))
        terms_ref[:, HALF - 128 :] += sums.T
        for n in range(HALF // STEP):
            y, r = divmod(i * (HALF // STEP) + n, OWNED // STEP)
            for t in range(TILES):
                o = t * (OWNED // STEP) + r
                block = terms_ref[n * STEP : (n + 1) * STEP, t * 128 : (t + 1) * 128]
                to = jnp.where(core == 0, y, o // 5)
                at = jnp.where(core == 0, o * STEP, y * QUARTER + o % 5 * STEP)
                at = pl.ds(pl.multiple_of(at, 16), STEP)
                order_ref[(to - place) & 3, at, :] = block
    own_ref[...] = order_ref[0]
    for by, ref in enumerate((out1_ref, out2_ref, out3_ref)):
        ref[...] = order_ref[by + 1].astype(jnp.bfloat16)


def products(core, grad0, grad1, rows0, rows1, sums):
    sent = jax.ShapeDtypeStruct((LINE, 128), jnp.bfloat16)
    return pl.pallas_call(
        product_kernel,
        out_shape=(jax.ShapeDtypeStruct((LINE, 128), jnp.float32), sent, sent, sent),
        in_specs=[SCALAR] + [ALL] * 5,
        out_specs=(ALL,) * 4,
        scratch_shapes=[
            pltpu.VMEM((HALF, HALF), jnp.float32),
            pltpu.VMEM((4, LINE, 128), jnp.float32),
        ],
        compiler_params=PARAMS,
        name="products",
    )(core, grad0, grad1, rows0, rows1, sums)


def fold_kernel(place_ref, own_ref, in1_ref, in2_ref, in3_ref, keep_ref, out1_ref, out2_ref, out3_ref, order_ref):
    place = place_ref[3]
    for d in range(4):
        at = slice(d * QUARTER, (d + 1) * QUARTER)
        block = own_ref[at, :]
        for ref in (in1_ref, in2_ref, in3_ref):
            block += ref[at, :].astype(jnp.float32)
        order_ref[(d - place) & 3] = block
    keep_ref[...] = order_ref[0]
    for by, ref in enumerate((out1_ref, out2_ref, out3_ref)):
        ref[...] = order_ref[by + 1].astype(jnp.bfloat16)


def fold(place, own, terms):
    sent = jax.ShapeDtypeStruct((QUARTER, 128), jnp.bfloat16)
    return pl.pallas_call(
        fold_kernel,
        out_shape=(jax.ShapeDtypeStruct((QUARTER, 128), jnp.float32), sent, sent, sent),
        in_specs=[SCALAR] + [ALL] * 4,
        out_specs=(ALL,) * 4,
        scratch_shapes=[pltpu.VMEM((4, QUARTER, 128), jnp.float32)],
        compiler_params=PARAMS,
        name="fold",
    )(place, own, *terms)


def runs():
    place = column_places()[0]
    found = []
    at = 0
    while at < KIN:
        stop = at + 1
        while stop < KIN and place[stop] == place[stop - 1] + 1 and place[stop] % 128 and stop % 128:
            stop += 1
        found.append((at, int(place[at]), stop - at))
        at = stop
    return found


def finish_kernel(place_ref, *refs):
    *parts, out_ref, norm_ref, held_ref, last_ref = refs
    core, x = place_ref[0], place_ref[4]
    for n, ref in enumerate(parts):
        side, by = divmod(n, 4)
        at = pl.multiple_of(((x - by) & 3) * QUARTER, 16)
        held_ref[core if side == 0 else 1 - core, pl.ds(at, QUARTER), :] = ref[...]
    lane = iota((OWNED, 128), 1)
    for tile in range(pl.cdiv(KIN, 128)):
        acc = None
        for at, src, size in runs():
            if at // 128 != tile:
                continue
            half, column = divmod(src // 128, TILES)
            piece = held_ref[half, column * OWNED : (column + 1) * OWNED, :]
            shift = (at - src) % 128
            if shift:
                piece = pltpu.roll(piece, shift, 1)
            acc = piece if acc is None else jnp.where(lane >= at % 128, piece, acc)
        width = min(128, KIN - tile * 128)
        out_ref[:, tile * 128 : tile * 128 + width] = acc[:, :width]
    last_ref[0:OWNED, :] = held_ref[0, LINE - OWNED :, :] + held_ref[1, LINE - OWNED :, :]
    last_ref[OWNED:, :] = jnp.zeros((384 - OWNED, 128), jnp.float32)
    norm_ref[...] = last_ref[...].T[SUMS : SUMS + 2, :OWNED]


def finish(place, parts):
    return pl.pallas_call(
        finish_kernel,
        out_shape=(
            jax.ShapeDtypeStruct((OWNED, KIN), jnp.float32),
            jax.ShapeDtypeStruct((2, OWNED), jnp.float32),
        ),
        in_specs=[SCALAR] + [ALL] * 8,
        out_specs=(ALL, ALL),
        scratch_shapes=[
            pltpu.VMEM((2, LINE, 128), jnp.float32),
            pltpu.VMEM((384, 128), jnp.float32),
        ],
        compiler_params=PARAMS,
        name="column_order",
    )(place, *parts)


def plane_index(core, x, y):
    return (core * 4 + x) * 4 + y


def plane_shift(by, along_y):
    pairs = []
    for x in range(4):
        for y in range(4):
            for core in range(2):
                to = (x, (y + by) % 4) if core == along_y else ((x + by) % 4, y)
                pairs.append((plane_index(core, x, y), plane_index(core, *to)))
    return pairs


def ring(by):
    return [(i, (i + by) % 4) for i in range(4)]


def copies(array, axis, count):
    array = jnp.broadcast_to(array[None], (count,) + array.shape)
    return lax.all_to_all(array, axis, 0, 0, tiled=True)


def shards(pixels, grad_norm, grad_resid, embed_weight, norm_gain, send_slot, recv_slot):
    plane = ("core", "slab", "fsdp")
    core = lax.axis_index("core").astype(jnp.int32)
    x = lax.axis_index("slab").astype(jnp.int32)
    y = lax.axis_index("fsdp").astype(jnp.int32)
    place = jnp.stack([core, jnp.where(core == 0, y, x), y, jnp.where(core == 0, x, y), x])
    earlier = lax.ppermute(pixels[:, :, 3:4], "slab", ring(1))
    takes = recv_slot.reshape(1, ROWS)
    sends = send_slot.reshape(ROWS, 1)
    packed0 = packed_rows(jnp.ones((1,), jnp.int32), takes, pixels, pixels, 0, 2)
    packed0, shard = lax.optimization_barrier((packed0, embed_weight))
    arrived0 = lax.all_to_all(packed0, ("z", "core"), 0, 0, tiled=True)
    swap = [(0, 1), (1, 0)]
    part = lax.dynamic_slice_in_dim(shard, core * (OWNED // 2), OWNED // 2, 0)
    parts = [lax.ppermute(part, "fsdp", ring(by)) for by in (1, 2, 3)]
    earlier, *parts = lax.optimization_barrier((earlier, *parts))
    packed1 = packed_rows((x > 0).astype(jnp.int32)[None], takes, earlier, pixels, 0, 1)
    arrived1 = lax.all_to_all(packed1, ("z", "core"), 0, 0, tiled=True)
    parts += [lax.ppermute(part, "core", swap) for part in parts]
    weight = padded_weight(place, embed_weight, parts)
    part = first_half(sends, arrived0, weight)
    grads, mine, send, sums = norm_backward(
        place, sends, arrived1, part, weight, grad_norm, grad_resid, norm_gain.reshape(1, D)
    )
    theirs = lax.ppermute(send, "core", swap)
    their_grads = lax.ppermute(grads, "core", swap)
    own, *sent = products(place, grads, their_grads, mine, theirs, sums)
    terms = [lax.ppermute(sent[by - 1], plane, plane_shift(by, 0)) for by in (1, 3, 2)]
    keep, *sent = fold(place, own, terms)
    terms = [lax.ppermute(sent[by - 1], plane, plane_shift(by, 1)) for by in (1, 3, 2)]
    quarter = keep + terms[0].astype(jnp.float32) + terms[1].astype(jnp.float32) + terms[2].astype(jnp.float32)
    quarter = jnp.pad(quarter, ((0, 8 * PIECE - QUARTER), (0, 0)))
    pieces = lax.all_to_all(quarter.reshape(8, PIECE, 128), "z", 0, 0, tiled=True)
    quarter = copies(jnp.sum(pieces, axis=0), "z", 8).reshape(8 * PIECE, 128)[:QUARTER]
    mine = [quarter] + [lax.ppermute(quarter, "slab", ring(by)) for by in (1, 2, 3)]
    return finish(place, mine + [lax.ppermute(part, "core", swap) for part in mine])


def solution(mesh):
    split = Mesh(mesh.devices.reshape(8, 2, 4, 4), ("z", "core", "slab", "fsdp"))
    dp = ("z", "core")
    return jax.shard_map(
        shards,
        mesh=split,
        in_specs=(
            P(dp, "fsdp", "slab", None, None, None),
            P("slab", "fsdp", dp, None),
            P("slab", "fsdp", dp, None),
            P("fsdp", None),
            P(),
            P("slab", "fsdp", dp),
            P("slab", "fsdp", dp),
        ),
        out_specs=(P("fsdp", None), P(None, "fsdp")),
        check_vma=False,
    )
```

```python
import jax
import jax.numpy as jnp
import numpy as np
from jax import lax
from jax.experimental import pallas as pl
from jax.experimental.pallas import tpu as pltpu
from jax.sharding import Mesh
from jax.sharding import PartitionSpec as P

GH = 16
GW = 16
PS = 14
COLOURS = 3
SIDE = 224
ROWS = 512
CAP = 64
PEERS = 16
D = 1280
KIN = 1176
GROUPS = 9
PARTS = COLOURS * PS
FRAME = PARTS * PS
HELD = 296
HALF = 640
TILES = HALF // 128
OWNED = D // 4
LINE = OWNED * TILES
QUARTER = LINE // 4
STEP = 80
PIECE = 56
BLOCK = 128
SUMS = 96
ALL = pl.BlockSpec(memory_space=pltpu.VMEM)
FAR = pl.BlockSpec(memory_space=pltpu.HBM)
SCALAR = pl.BlockSpec(memory_space=pltpu.SMEM)
PARAMS = pltpu.CompilerParams(vmem_limit_bytes=24 * 1024 * 1024)
NORM = pltpu.CompilerParams(vmem_limit_bytes=49 * 1024 * 1024)
WIDE = pltpu.CompilerParams(vmem_limit_bytes=60 * 1024 * 1024)
LANES = (((1,), (1,)), ((), ()))
SUBLANES = (((0,), (0,)), ((), ()))


def one_hot(match):
    return match.astype(jnp.float32).astype(jnp.bfloat16)


def iota(shape, dim):
    return lax.broadcasted_iota(jnp.int32, shape, dim)


def dot(a, b, dims=(((1,), (0,)), ((), ()))):
    return lax.dot_general(a, b, dims, preferred_element_type=jnp.float32)


def column_places():
    place = np.zeros((1, KIN), np.int32)
    for c in range(COLOURS):
        for t in range(2):
            part = c * PS * PS + np.arange(PS * PS)
            at = (c * 2 + t) * PS * PS
            place[0, at : at + PS * PS] = (1 - t) * HALF + part
    return place


def patch_kernel(valid_ref, slot_ref, fa_ref, fb_ref, out_ref, spread_ref, rows_ref):
    src = iota((SIDE, 256), 0)
    place = jnp.where(src >= GROUPS * PS, src + 2, src)
    spread = one_hot(iota((SIDE, 256), 1) == place)
    for k, ref in enumerate((fa_ref, fb_ref)):
        for c in range(COLOURS):
            wide = dot(ref[0, 0, 0, c], spread)
            for h in range(2):
                spread_ref[k, c, h] = wide[:, h * 128 : (h + 1) * 128]

    @pl.when(valid_ref[0] == 0)
    def _():
        spread_ref[0] = jnp.zeros_like(spread_ref[0])

    lane = iota((GH, 128), 1)
    for k in range(2):
        for x in range(GW):
            here = slice((k * GW + x) * GH, (k * GW + x + 1) * GH)
            acc = None
            for n in range(PARTS):
                c, p = divmod(n, PS)
                piece = spread_ref[k, c, x // GROUPS, pl.ds(p, GH, stride=PS), :]
                shift = PS * (n - x % GROUPS) % 128
                if shift:
                    piece = pltpu.roll(piece, shift, 1)
                tile, at = divmod(PS * n, 128)
                acc = piece if acc is None else jnp.where(lane >= at, piece, acc)
                if n == PARTS - 1:
                    acc = jnp.where(lane < at + PS, acc, 0.0)
                if at + PS >= 128 or n == PARTS - 1:
                    rows_ref[here, tile * 128 : (tile + 1) * 128] = acc.astype(jnp.bfloat16)
                    acc = piece
    slots = slot_ref[...]
    kind = iota((16, ROWS), 0)
    digits = jnp.where(kind == 0, slots >> 6, jnp.where(kind == 1, slots & 63, 0))
    dst = iota((ROWS, ROWS), 0)
    order = one_hot(iota((ROWS, ROWS), 1) == (dst & 256) + ((dst & 15) << 4) + ((dst >> 4) & 15))
    digits = dot(order, digits.astype(jnp.float32).astype(jnp.bfloat16), LANES)
    slots = (digits[:, 0:1] * 64.0 + digits[:, 1:2]).astype(jnp.int32)
    side = iota((HELD, 128), 1) < CAP
    for i in range(PEERS // 4):
        pick = one_hot(iota((ROWS, 256), 1) + i * 256 == slots)
        both = dot(rows_ref[...], pick, SUBLANES)
        for j in range(2):
            lo = both[0:HELD, j * 128 : (j + 1) * 128]
            hi = both[HELD : 2 * HELD, j * 128 : (j + 1) * 128]
            peer = i * 4 + j * 2
            out_ref[peer] = jnp.where(side, lo, pltpu.roll(hi, CAP, 1)).astype(jnp.bfloat16)
            out_ref[peer + 1] = jnp.where(side, pltpu.roll(lo, CAP, 1), hi).astype(jnp.bfloat16)


def packed_rows(valid, slots, first, second, first_at, second_at):
    block = (1, 1, 1, COLOURS, SIDE, SIDE)
    shape = (PEERS, HELD, 128)
    return pl.pallas_call(
        patch_kernel,
        out_shape=jax.ShapeDtypeStruct(shape, jnp.bfloat16),
        grid=(1,),
        in_specs=[
            SCALAR,
            pl.BlockSpec((1, ROWS), lambda i: (0, 0)),
            pl.BlockSpec(block, lambda i: (0, 0, first_at, 0, 0, 0)),
            pl.BlockSpec(block, lambda i: (0, 0, second_at, 0, 0, 0)),
        ],
        out_specs=pl.BlockSpec(shape, lambda i: (0, 0, 0)),
        scratch_shapes=[
            pltpu.VMEM((2, COLOURS, 2, SIDE, 128), jnp.float32),
            pltpu.VMEM((ROWS, HALF), jnp.bfloat16),
        ],
        compiler_params=WIDE,
        name="patch_rows",
    )(valid, slots, first, second)


def weight_kernel(place_ref, column_ref, own_ref, *refs):
    *parts, out_ref, held_ref = refs
    core, y = place_ref[0], place_ref[2]
    part = OWNED // 2
    held_ref[pl.ds(pl.multiple_of(y * OWNED, 16), OWNED), :] = own_ref[...]
    for n, ref in enumerate(parts):
        side, by = divmod(n, 3)
        row = ((y - by - 1) & 3) * OWNED + (core if side == 0 else 1 - core) * part
        held_ref[pl.ds(pl.multiple_of(row, 16), part), :] = ref[...]
    for i in range(2):
        pick = one_hot(iota((HALF, KIN), 0) + i * HALF == column_ref[...])
        out_ref[:, i * HALF : (i + 1) * HALF] = dot(held_ref[...], pick, LANES).astype(jnp.bfloat16)


def padded_weight(place, own, parts):
    return pl.pallas_call(
        weight_kernel,
        out_shape=jax.ShapeDtypeStruct((D, 2 * HALF), jnp.bfloat16),
        in_specs=[SCALAR] + [ALL] * 8,
        out_specs=ALL,
        scratch_shapes=[pltpu.VMEM((D, KIN), jnp.bfloat16)],
        compiler_params=WIDE,
        name="weight_columns",
    )(place, jnp.asarray(column_places()), own, *parts)


def taken_rows(slot_ref, arr_ref, cols_ref):
    side = iota((HELD, 128), 1) < CAP
    for j in range(PEERS // 2):
        even = arr_ref[2 * j].astype(jnp.float32)
        odd = arr_ref[2 * j + 1].astype(jnp.float32)
        low = jnp.where(side, even, pltpu.roll(odd, CAP, 1))
        high = jnp.where(side, pltpu.roll(even, CAP, 1), odd)
        both = jnp.concatenate([low, high], axis=0).astype(jnp.bfloat16)
        cols_ref[: 2 * HELD, j * 128 : (j + 1) * 128] = both
    cols_ref[2 * HELD :, :] = jnp.zeros((HALF - 2 * HELD, PEERS * CAP), jnp.bfloat16)
    pick = one_hot(iota((ROWS, PEERS * CAP), 1) == slot_ref[...])
    return dot(pick, cols_ref[...], LANES).astype(jnp.bfloat16)


def first_kernel(slot_ref, arr_ref, w_ref, part_ref, cols_ref, rows_ref):
    rows_ref[...] = taken_rows(slot_ref, arr_ref, cols_ref)

    def block(i, carry):
        here = pl.ds(pl.multiple_of(i * 128, 128), 128)
        part_ref[here, :D] = dot(rows_ref[here, :], w_ref[:, :HALF], LANES)
        part_ref[here, D:] = rows_ref[here, :].astype(jnp.float32)
        return carry

    lax.fori_loop(0, ROWS // 128, block, 0)


def first_half(slots, arrived, weight):
    return pl.pallas_call(
        first_kernel,
        out_shape=jax.ShapeDtypeStruct((ROWS, D + HALF), jnp.float32),
        in_specs=[ALL] * 3,
        out_specs=ALL,
        scratch_shapes=[
            pltpu.VMEM((HALF, PEERS * CAP), jnp.bfloat16),
            pltpu.VMEM((ROWS, HALF), jnp.bfloat16),
        ],
        compiler_params=WIDE,
        name="first_half",
    )(slots, arrived, weight)


def backward_kernel(core_ref, slot_ref, arr_ref, part_far, w_far, g_far, r_far, gain_ref, grad_ref, mine_ref, send_ref, sums_ref, cols_ref, rows1_ref, part_ref, w_ref, g_ref, r_ref, sems):
    reads = [
        pltpu.make_async_copy(w_far.at[:, HALF:], w_ref, sems.at[0]),
        pltpu.make_async_copy(part_far, part_ref, sems.at[1]),
        pltpu.make_async_copy(g_far.at[0, 0], g_ref, sems.at[2]),
        pltpu.make_async_copy(r_far.at[0, 0], r_ref, sems.at[3]),
    ]
    for read in reads:
        read.start()
    rows1_ref[...] = taken_rows(slot_ref, arr_ref, cols_ref)
    for read in reads:
        read.wait()

    @pl.when(core_ref[0] == 0)
    def _():
        mine_ref[...] = part_ref[:, D:].astype(jnp.bfloat16)
        send_ref[...] = rows1_ref[...]

    @pl.when(core_ref[0] != 0)
    def _():
        mine_ref[...] = rows1_ref[...]
        send_ref[...] = part_ref[:, D:].astype(jnp.bfloat16)

    sums_ref[...] = jnp.zeros_like(sums_ref)

    def block(i, carry):
        here = pl.ds(pl.multiple_of(i * BLOCK, BLOCK), BLOCK)
        embedded = part_ref[here, :D] + dot(rows1_ref[here, :], w_ref[...], LANES)
        deviation = embedded - jnp.mean(embedded, axis=-1, keepdims=True)
        variance = jnp.mean(deviation * deviation, axis=-1, keepdims=True)
        inverse_std = lax.rsqrt(variance + 1e-06)
        normalized = deviation * inverse_std
        upstream_norm = g_ref[here, :].astype(jnp.float32)
        upstream = upstream_norm * gain_ref[...]
        inner = jnp.mean(upstream * normalized, axis=-1, keepdims=True)
        level = jnp.mean(upstream, axis=-1, keepdims=True)
        input_grad = r_ref[here, :].astype(jnp.float32) + inverse_std * (
            upstream - level - normalized * inner
        )
        grad_ref[here, :] = input_grad.astype(jnp.bfloat16)
        sums_ref[0:8, :] += jnp.sum((upstream_norm * normalized).reshape(BLOCK // 8, 8, D), axis=0)
        sums_ref[8:16, :] += jnp.sum(upstream_norm.reshape(BLOCK // 8, 8, D), axis=0)
        return carry

    lax.fori_loop(0, ROWS // BLOCK, block, 0)


def norm_backward(core, slots, arrived, part, weight, grad_norm, grad_resid, gain):
    half = jax.ShapeDtypeStruct((ROWS, HALF), jnp.bfloat16)
    return pl.pallas_call(
        backward_kernel,
        out_shape=(
            jax.ShapeDtypeStruct((ROWS, D), jnp.bfloat16),
            half,
            half,
            jax.ShapeDtypeStruct((16, D), jnp.float32),
        ),
        in_specs=[SCALAR, ALL, ALL, FAR, FAR, FAR, FAR, ALL],
        out_specs=(ALL,) * 4,
        scratch_shapes=[
            pltpu.VMEM((HALF, PEERS * CAP), jnp.bfloat16),
            pltpu.VMEM((ROWS, HALF), jnp.bfloat16),
            pltpu.VMEM((ROWS, D + HALF), jnp.float32),
            pltpu.VMEM((D, HALF), jnp.bfloat16),
            pltpu.VMEM((ROWS, D), jnp.bfloat16),
            pltpu.VMEM((ROWS, D), jnp.bfloat16),
            pltpu.SemaphoreType.DMA((4,)),
        ],
        compiler_params=NORM,
        name="norm_backward",
    )(core, slots, arrived, part, weight, grad_norm, grad_resid, gain)


def product_kernel(core_ref, grad0_ref, grad1_ref, rows0_ref, rows1_ref, sums_ref, own_ref, out1_ref, out2_ref, out3_ref, terms_ref, order_ref):
    core, place = core_ref[0], core_ref[1]
    kind = iota((128, HALF), 0)
    for i in range(D // HALF):
        here = slice(i * HALF, (i + 1) * HALF)
        terms_ref[...] = dot(grad0_ref[:, here], rows0_ref[...], SUBLANES) + dot(
            grad1_ref[:, here], rows1_ref[...], SUBLANES
        )
        gain_sum = jnp.sum(sums_ref[0:8, here], axis=0, keepdims=True)
        bias_sum = jnp.sum(sums_ref[8:16, here], axis=0, keepdims=True)
        sums = jnp.where(kind == SUMS, gain_sum, jnp.where(kind == SUMS + 1, bias_sum, 0.0))
        terms_ref[:, HALF - 128 :] += sums.T
        for n in range(HALF // STEP):
            y, r = divmod(i * (HALF // STEP) + n, OWNED // STEP)
            for t in range(TILES):
                o = t * (OWNED // STEP) + r
                block = terms_ref[n * STEP : (n + 1) * STEP, t * 128 : (t + 1) * 128]
                to = jnp.where(core == 0, y, o // 5)
                at = jnp.where(core == 0, o * STEP, y * QUARTER + o % 5 * STEP)
                at = pl.ds(pl.multiple_of(at, 16), STEP)
                order_ref[(to - place) & 3, at, :] = block
    own_ref[...] = order_ref[0]
    for by, ref in enumerate((out1_ref, out2_ref, out3_ref)):
        ref[...] = order_ref[by + 1].astype(jnp.bfloat16)


def products(core, grad0, grad1, rows0, rows1, sums):
    sent = jax.ShapeDtypeStruct((LINE, 128), jnp.bfloat16)
    return pl.pallas_call(
        product_kernel,
        out_shape=(jax.ShapeDtypeStruct((LINE, 128), jnp.float32), sent, sent, sent),
        in_specs=[SCALAR] + [ALL] * 5,
        out_specs=(ALL,) * 4,
        scratch_shapes=[
            pltpu.VMEM((HALF, HALF), jnp.float32),
            pltpu.VMEM((4, LINE, 128), jnp.float32),
        ],
        compiler_params=PARAMS,
        name="products",
    )(core, grad0, grad1, rows0, rows1, sums)


def fold_kernel(place_ref, own_ref, in1_ref, in2_ref, in3_ref, keep_ref, out1_ref, out2_ref, out3_ref, order_ref):
    place = place_ref[3]
    for d in range(4):
        at = slice(d * QUARTER, (d + 1) * QUARTER)
        block = own_ref[at, :]
        for ref in (in1_ref, in2_ref, in3_ref):
            block += ref[at, :].astype(jnp.float32)
        order_ref[(d - place) & 3] = block
    keep_ref[...] = order_ref[0]
    for by, ref in enumerate((out1_ref, out2_ref, out3_ref)):
        ref[...] = order_ref[by + 1].astype(jnp.bfloat16)


def fold(place, own, terms):
    sent = jax.ShapeDtypeStruct((QUARTER, 128), jnp.bfloat16)
    return pl.pallas_call(
        fold_kernel,
        out_shape=(jax.ShapeDtypeStruct((QUARTER, 128), jnp.float32), sent, sent, sent),
        in_specs=[SCALAR] + [ALL] * 4,
        out_specs=(ALL,) * 4,
        scratch_shapes=[pltpu.VMEM((4, QUARTER, 128), jnp.float32)],
        compiler_params=PARAMS,
        name="fold",
    )(place, own, *terms)


def runs():
    place = column_places()[0]
    found = []
    at = 0
    while at < KIN:
        stop = at + 1
        while stop < KIN and place[stop] == place[stop - 1] + 1 and place[stop] % 128 and stop % 128:
            stop += 1
        found.append((at, int(place[at]), stop - at))
        at = stop
    return found


def finish_kernel(place_ref, *refs):
    *parts, out_ref, norm_ref, held_ref, last_ref = refs
    core, x = place_ref[0], place_ref[4]
    for n, ref in enumerate(parts):
        side, by = divmod(n, 4)
        at = pl.multiple_of(((x - by) & 3) * QUARTER, 16)
        held_ref[core if side == 0 else 1 - core, pl.ds(at, QUARTER), :] = ref[...]
    lane = iota((OWNED, 128), 1)
    for tile in range(pl.cdiv(KIN, 128)):
        acc = None
        for at, src, size in runs():
            if at // 128 != tile:
                continue
            half, column = divmod(src // 128, TILES)
            piece = held_ref[half, column * OWNED : (column + 1) * OWNED, :]
            shift = (at - src) % 128
            if shift:
                piece = pltpu.roll(piece, shift, 1)
            acc = piece if acc is None else jnp.where(lane >= at % 128, piece, acc)
        width = min(128, KIN - tile * 128)
        out_ref[:, tile * 128 : tile * 128 + width] = acc[:, :width]
    last_ref[0:OWNED, :] = held_ref[0, LINE - OWNED :, :] + held_ref[1, LINE - OWNED :, :]
    last_ref[OWNED:, :] = jnp.zeros((384 - OWNED, 128), jnp.float32)
    norm_ref[...] = last_ref[...].T[SUMS : SUMS + 2, :OWNED]


def finish(place, parts):
    return pl.pallas_call(
        finish_kernel,
        out_shape=(
            jax.ShapeDtypeStruct((OWNED, KIN), jnp.float32),
            jax.ShapeDtypeStruct((2, OWNED), jnp.float32),
        ),
        in_specs=[SCALAR] + [ALL] * 8,
        out_specs=(ALL, ALL),
        scratch_shapes=[
            pltpu.VMEM((2, LINE, 128), jnp.float32),
            pltpu.VMEM((384, 128), jnp.float32),
        ],
        compiler_params=PARAMS,
        name="column_order",
    )(place, *parts)


def plane_index(core, x, y):
    return (core * 4 + x) * 4 + y


def plane_shift(by, along_y):
    pairs = []
    for x in range(4):
        for y in range(4):
            for core in range(2):
                to = (x, (y + by) % 4) if core == along_y else ((x + by) % 4, y)
                pairs.append((plane_index(core, x, y), plane_index(core, *to)))
    return pairs


def ring(by):
    return [(i, (i + by) % 4) for i in range(4)]


def copies(array, axis, count):
    array = jnp.broadcast_to(array[None], (count,) + array.shape)
    return lax.all_to_all(array, axis, 0, 0, tiled=True)


def shards(pixels, grad_norm, grad_resid, embed_weight, norm_gain, send_slot, recv_slot):
    plane = ("core", "slab", "fsdp")
    core = lax.axis_index("core").astype(jnp.int32)
    x = lax.axis_index("slab").astype(jnp.int32)
    y = lax.axis_index("fsdp").astype(jnp.int32)
    place = jnp.stack([core, jnp.where(core == 0, y, x), y, jnp.where(core == 0, x, y), x])
    earlier = lax.ppermute(pixels[:, :, 3:4], "slab", ring(1))
    takes = recv_slot.reshape(1, ROWS)
    sends = send_slot.reshape(ROWS, 1)
    packed0 = packed_rows(jnp.ones((1,), jnp.int32), takes, pixels, pixels, 0, 2)
    packed0, shard = lax.optimization_barrier((packed0, embed_weight))
    arrived0 = lax.all_to_all(packed0, ("z", "core"), 0, 0, tiled=True)
    swap = [(0, 1), (1, 0)]
    part = lax.dynamic_slice_in_dim(shard, core * (OWNED // 2), OWNED // 2, 0)
    parts = [lax.ppermute(part, "fsdp", ring(by)) for by in (1, 2, 3)]
    earlier, *parts = lax.optimization_barrier((earlier, *parts))
    packed1 = packed_rows((x > 0).astype(jnp.int32)[None], takes, earlier, pixels, 0, 1)
    arrived1 = lax.all_to_all(packed1, ("z", "core"), 0, 0, tiled=True)
    parts += [lax.ppermute(part, "core", swap) for part in parts]
    weight = padded_weight(place, embed_weight, parts)
    part = first_half(sends, arrived0, weight)
    grads, mine, send, sums = norm_backward(
        place, sends, arrived1, part, weight, grad_norm, grad_resid, norm_gain.reshape(1, D)
    )
    theirs = lax.ppermute(send, "core", swap)
    their_grads = lax.ppermute(grads, "core", swap)
    own, *sent = products(place, grads, their_grads, mine, theirs, sums)
    terms = [lax.ppermute(sent[by - 1], plane, plane_shift(by, 0)) for by in (1, 3, 2)]
    keep, *sent = fold(place, own, terms)
    terms = [lax.ppermute(sent[by - 1], plane, plane_shift(by, 1)) for by in (1, 3, 2)]
    quarter = keep + terms[0].astype(jnp.float32) + terms[1].astype(jnp.float32) + terms[2].astype(jnp.float32)
    quarter = jnp.pad(quarter, ((0, 8 * PIECE - QUARTER), (0, 0)))
    pieces = lax.all_to_all(quarter.reshape(8, PIECE, 128), "z", 0, 0, tiled=True)
    quarter = copies(jnp.sum(pieces, axis=0), "z", 8).reshape(8 * PIECE, 128)[:QUARTER]
    mine = [quarter] + [lax.ppermute(quarter, "slab", ring(by)) for by in (1, 2, 3)]
    return finish(place, mine + [lax.ppermute(part, "core", swap) for part in mine])


def solution(mesh):
    split = Mesh(mesh.devices.reshape(8, 2, 4, 4), ("z", "core", "slab", "fsdp"))
    dp = ("z", "core")
    return jax.shard_map(
        shards,
        mesh=split,
        in_specs=(
            P(dp, "fsdp", "slab", None, None, None),
            P("slab", "fsdp", dp, None),
            P("slab", "fsdp", dp, None),
            P("fsdp", None),
            P(),
            P("slab", "fsdp", dp),
            P("slab", "fsdp", dp),
        ),
        out_specs=(P("fsdp", None), P(None, "fsdp")),
        check_vma=False,
    )
```

```python
import jax
import jax.numpy as jnp
import numpy as np
from jax import lax
from jax.experimental import pallas as pl
from jax.experimental.pallas import tpu as pltpu
from jax.sharding import Mesh
from jax.sharding import PartitionSpec as P

GH = 16
GW = 16
PS = 14
COLOURS = 3
SIDE = 224
ROWS = 512
CAP = 64
PEERS = 16
D = 1280
KIN = 1176
GROUPS = 9
PARTS = COLOURS * PS
FRAME = PARTS * PS
HELD = 296
HALF = 640
TILES = HALF // 128
OWNED = D // 4
LINE = OWNED * TILES
QUARTER = LINE // 4
STEP = 80
PIECE = 56
BLOCK = 256
SUMS = 96
ALL = pl.BlockSpec(memory_space=pltpu.VMEM)
FAR = pl.BlockSpec(memory_space=pltpu.HBM)
SCALAR = pl.BlockSpec(memory_space=pltpu.SMEM)
PARAMS = pltpu.CompilerParams(vmem_limit_bytes=24 * 1024 * 1024)
NORM = pltpu.CompilerParams(vmem_limit_bytes=49 * 1024 * 1024)
WIDE = pltpu.CompilerParams(vmem_limit_bytes=60 * 1024 * 1024)
LANES = (((1,), (1,)), ((), ()))
SUBLANES = (((0,), (0,)), ((), ()))


def one_hot(match):
    return match.astype(jnp.float32).astype(jnp.bfloat16)


def iota(shape, dim):
    return lax.broadcasted_iota(jnp.int32, shape, dim)


def dot(a, b, dims=(((1,), (0,)), ((), ()))):
    return lax.dot_general(a, b, dims, preferred_element_type=jnp.float32)


def column_places():
    place = np.zeros((1, KIN), np.int32)
    for c in range(COLOURS):
        for t in range(2):
            part = c * PS * PS + np.arange(PS * PS)
            at = (c * 2 + t) * PS * PS
            place[0, at : at + PS * PS] = (1 - t) * HALF + part
    return place


def patch_kernel(valid_ref, slot_ref, fa_ref, fb_ref, out_ref, spread_ref, rows_ref):
    src = iota((SIDE, 256), 0)
    place = jnp.where(src >= GROUPS * PS, src + 2, src)
    spread = one_hot(iota((SIDE, 256), 1) == place)
    for k, ref in enumerate((fa_ref, fb_ref)):
        for c in range(COLOURS):
            wide = dot(ref[0, 0, 0, c], spread)
            for h in range(2):
                spread_ref[k, c, h, :SIDE] = wide[:, h * 128 : (h + 1) * 128]

    @pl.when(valid_ref[0] == 0)
    def _():
        spread_ref[0] = jnp.zeros_like(spread_ref[0])

    lane = iota((GH, 128), 1)
    for k in range(2):
        for x in range(GW):
            here = slice((k * GW + x) * GH, (k * GW + x + 1) * GH)
            acc = None
            for n in range(PARTS):
                c, p = divmod(n, PS)
                piece = spread_ref[k, c, x // GROUPS, pl.ds(p, GH, stride=PS), :]
                shift = PS * (n - x % GROUPS) % 128
                if shift:
                    piece = pltpu.roll(piece, shift, 1)
                tile, at = divmod(PS * n, 128)
                acc = piece if acc is None else jnp.where(lane >= at, piece, acc)
                if n == PARTS - 1:
                    acc = jnp.where(lane < at + PS, acc, 0.0)
                if at + PS >= 128 or n == PARTS - 1:
                    rows_ref[here, tile * 128 : (tile + 1) * 128] = acc.astype(jnp.bfloat16)
                    acc = piece
    slots = slot_ref[...]
    kind = iota((16, ROWS), 0)
    digits = jnp.where(kind == 0, slots >> 6, jnp.where(kind == 1, slots & 63, 0))
    dst = iota((ROWS, ROWS), 0)
    order = one_hot(iota((ROWS, ROWS), 1) == (dst & 256) + ((dst & 15) << 4) + ((dst >> 4) & 15))
    digits = dot(order, digits.astype(jnp.float32).astype(jnp.bfloat16), LANES)
    slots = (digits[:, 0:1] * 64.0 + digits[:, 1:2]).astype(jnp.int32)
    side = iota((HELD, 128), 1) < CAP
    for i in range(PEERS // 4):
        pick = one_hot(iota((ROWS, 256), 1) + i * 256 == slots)
        both = dot(rows_ref[...], pick, SUBLANES)
        for j in range(2):
            lo = both[0:HELD, j * 128 : (j + 1) * 128]
            hi = both[HELD : 2 * HELD, j * 128 : (j + 1) * 128]
            peer = i * 4 + j * 2
            out_ref[peer] = jnp.where(side, lo, pltpu.roll(hi, CAP, 1)).astype(jnp.bfloat16)
            out_ref[peer + 1] = jnp.where(side, pltpu.roll(lo, CAP, 1), hi).astype(jnp.bfloat16)


def packed_rows(valid, slots, first, second, first_at, second_at):
    block = (1, 1, 1, COLOURS, SIDE, SIDE)
    shape = (PEERS, HELD, 128)
    return pl.pallas_call(
        patch_kernel,
        out_shape=jax.ShapeDtypeStruct(shape, jnp.bfloat16),
        grid=(1,),
        in_specs=[
            SCALAR,
            pl.BlockSpec((1, ROWS), lambda i: (0, 0)),
            pl.BlockSpec(block, lambda i: (0, 0, first_at, 0, 0, 0)),
            pl.BlockSpec(block, lambda i: (0, 0, second_at, 0, 0, 0)),
        ],
        out_specs=pl.BlockSpec(shape, lambda i: (0, 0, 0)),
        scratch_shapes=[
            pltpu.VMEM((2, COLOURS, 2, GH * (PS + 1), 128), jnp.float32),
            pltpu.VMEM((ROWS, HALF), jnp.bfloat16),
        ],
        compiler_params=WIDE,
        name="patch_rows",
    )(valid, slots, first, second)


def weight_kernel(place_ref, column_ref, own_ref, *refs):
    *parts, out_ref, held_ref = refs
    core, y = place_ref[0], place_ref[2]
    part = OWNED // 2
    held_ref[pl.ds(pl.multiple_of(y * OWNED, 16), OWNED), :] = own_ref[...]
    for n, ref in enumerate(parts):
        side, by = divmod(n, 3)
        row = ((y - by - 1) & 3) * OWNED + (core if side == 0 else 1 - core) * part
        held_ref[pl.ds(pl.multiple_of(row, 16), part), :] = ref[...]
    for i in range(2):
        pick = one_hot(iota((HALF, KIN), 0) + i * HALF == column_ref[...])
        out_ref[:, i * HALF : (i + 1) * HALF] = dot(held_ref[...], pick, LANES).astype(jnp.bfloat16)


def padded_weight(place, own, parts):
    return pl.pallas_call(
        weight_kernel,
        out_shape=jax.ShapeDtypeStruct((D, 2 * HALF), jnp.bfloat16),
        in_specs=[SCALAR] + [ALL] * 8,
        out_specs=ALL,
        scratch_shapes=[pltpu.VMEM((D, KIN), jnp.bfloat16)],
        compiler_params=WIDE,
        name="weight_columns",
    )(place, jnp.asarray(column_places()), own, *parts)


def taken_rows(slot_ref, arr_ref, cols_ref):
    side = iota((HELD, 128), 1) < CAP
    for j in range(PEERS // 2):
        even = arr_ref[2 * j].astype(jnp.float32)
        odd = arr_ref[2 * j + 1].astype(jnp.float32)
        low = jnp.where(side, even, pltpu.roll(odd, CAP, 1))
        high = jnp.where(side, pltpu.roll(even, CAP, 1), odd)
        both = jnp.concatenate([low, high], axis=0).astype(jnp.bfloat16)
        cols_ref[: 2 * HELD, j * 128 : (j + 1) * 128] = both
    cols_ref[2 * HELD :, :] = jnp.zeros((HALF - 2 * HELD, PEERS * CAP), jnp.bfloat16)
    pick = one_hot(iota((ROWS, PEERS * CAP), 1) == slot_ref[...])
    return dot(pick, cols_ref[...], LANES).astype(jnp.bfloat16)


def first_kernel(slot_ref, arr_ref, w_ref, part_ref, cols_ref, rows_ref):
    rows_ref[...] = taken_rows(slot_ref, arr_ref, cols_ref)

    def block(i, carry):
        here = pl.ds(pl.multiple_of(i * 128, 128), 128)
        part_ref[here, :D] = dot(rows_ref[here, :], w_ref[:, :HALF], LANES)
        part_ref[here, D:] = rows_ref[here, :].astype(jnp.float32)
        return carry

    lax.fori_loop(0, ROWS // 128, block, 0)


def first_half(slots, arrived, weight):
    return pl.pallas_call(
        first_kernel,
        out_shape=jax.ShapeDtypeStruct((ROWS, D + HALF), jnp.float32),
        in_specs=[ALL] * 3,
        out_specs=ALL,
        scratch_shapes=[
            pltpu.VMEM((HALF, PEERS * CAP), jnp.bfloat16),
            pltpu.VMEM((ROWS, HALF), jnp.bfloat16),
        ],
        compiler_params=WIDE,
        name="first_half",
    )(slots, arrived, weight)


def backward_kernel(core_ref, slot_ref, arr_ref, part_far, w_far, g_far, r_far, gain_ref, grad_ref, mine_ref, send_ref, sums_ref, cols_ref, rows1_ref, part_ref, w_ref, g_ref, r_ref, sems):
    reads = [
        pltpu.make_async_copy(w_far.at[:, HALF:], w_ref, sems.at[0]),
        pltpu.make_async_copy(part_far, part_ref, sems.at[1]),
        pltpu.make_async_copy(g_far.at[0, 0], g_ref, sems.at[2]),
        pltpu.make_async_copy(r_far.at[0, 0], r_ref, sems.at[3]),
    ]
    for read in reads:
        read.start()
    rows1_ref[...] = taken_rows(slot_ref, arr_ref, cols_ref)
    for read in reads:
        read.wait()

    @pl.when(core_ref[0] == 0)
    def _():
        mine_ref[...] = part_ref[:, D:].astype(jnp.bfloat16)
        send_ref[...] = rows1_ref[...]

    @pl.when(core_ref[0] != 0)
    def _():
        mine_ref[...] = rows1_ref[...]
        send_ref[...] = part_ref[:, D:].astype(jnp.bfloat16)

    sums_ref[...] = jnp.zeros_like(sums_ref)
    for i in range(D // 256):
        at = slice(i * 256, (i + 1) * 256)
        part_ref[:, at] += dot(rows1_ref[...], w_ref[at, :], LANES)

    def block(i, carry):
        here = pl.ds(pl.multiple_of(i * BLOCK, BLOCK), BLOCK)
        embedded = part_ref[here, :D]
        deviation = embedded - jnp.mean(embedded, axis=-1, keepdims=True)
        variance = jnp.mean(deviation * deviation, axis=-1, keepdims=True)
        inverse_std = lax.rsqrt(variance + 1e-06)
        normalized = deviation * inverse_std
        upstream_norm = g_ref[here, :].astype(jnp.float32)
        upstream = upstream_norm * gain_ref[...]
        inner = jnp.mean(upstream * normalized, axis=-1, keepdims=True)
        level = jnp.mean(upstream, axis=-1, keepdims=True)
        input_grad = r_ref[here, :].astype(jnp.float32) + inverse_std * (
            upstream - level - normalized * inner
        )
        grad_ref[here, :] = input_grad.astype(jnp.bfloat16)
        sums_ref[0:8, :] += jnp.sum((upstream_norm * normalized).reshape(BLOCK // 8, 8, D), axis=0)
        sums_ref[8:16, :] += jnp.sum(upstream_norm.reshape(BLOCK // 8, 8, D), axis=0)
        return carry

    lax.fori_loop(0, ROWS // BLOCK, block, 0)


def norm_backward(core, slots, arrived, part, weight, grad_norm, grad_resid, gain):
    half = jax.ShapeDtypeStruct((ROWS, HALF), jnp.bfloat16)
    return pl.pallas_call(
        backward_kernel,
        out_shape=(
            jax.ShapeDtypeStruct((ROWS, D), jnp.bfloat16),
            half,
            half,
            jax.ShapeDtypeStruct((16, D), jnp.float32),
        ),
        in_specs=[SCALAR, ALL, ALL, FAR, FAR, FAR, FAR, ALL],
        out_specs=(ALL,) * 4,
        scratch_shapes=[
            pltpu.VMEM((HALF, PEERS * CAP), jnp.bfloat16),
            pltpu.VMEM((ROWS, HALF), jnp.bfloat16),
            pltpu.VMEM((ROWS, D + HALF), jnp.float32),
            pltpu.VMEM((D, HALF), jnp.bfloat16),
            pltpu.VMEM((ROWS, D), jnp.bfloat16),
            pltpu.VMEM((ROWS, D), jnp.bfloat16),
            pltpu.SemaphoreType.DMA((4,)),
        ],
        compiler_params=NORM,
        name="norm_backward",
    )(core, slots, arrived, part, weight, grad_norm, grad_resid, gain)


def product_kernel(core_ref, grad0_ref, grad1_ref, rows0_ref, rows1_ref, sums_ref, own_ref, out1_ref, out2_ref, out3_ref, terms_ref, order_ref):
    core, place = core_ref[0], core_ref[1]
    kind = iota((128, HALF), 0)
    for i in range(D // HALF):
        here = slice(i * HALF, (i + 1) * HALF)
        terms_ref[...] = dot(grad0_ref[:, here], rows0_ref[...], SUBLANES) + dot(
            grad1_ref[:, here], rows1_ref[...], SUBLANES
        )
        gain_sum = jnp.sum(sums_ref[0:8, here], axis=0, keepdims=True)
        bias_sum = jnp.sum(sums_ref[8:16, here], axis=0, keepdims=True)
        sums = jnp.where(kind == SUMS, gain_sum, jnp.where(kind == SUMS + 1, bias_sum, 0.0))
        terms_ref[:, HALF - 128 :] += sums.T
        for n in range(HALF // STEP):
            y, r = divmod(i * (HALF // STEP) + n, OWNED // STEP)
            for t in range(TILES):
                o = t * (OWNED // STEP) + r
                block = terms_ref[n * STEP : (n + 1) * STEP, t * 128 : (t + 1) * 128]
                to = jnp.where(core == 0, y, o // 5)
                at = jnp.where(core == 0, o * STEP, y * QUARTER + o % 5 * STEP)
                at = pl.ds(pl.multiple_of(at, 16), STEP)
                order_ref[(to - place) & 3, at, :] = block
    own_ref[...] = order_ref[0]
    for by, ref in enumerate((out1_ref, out2_ref, out3_ref)):
        ref[...] = order_ref[by + 1].astype(jnp.bfloat16)


def products(core, grad0, grad1, rows0, rows1, sums):
    sent = jax.ShapeDtypeStruct((LINE, 128), jnp.bfloat16)
    return pl.pallas_call(
        product_kernel,
        out_shape=(jax.ShapeDtypeStruct((LINE, 128), jnp.float32), sent, sent, sent),
        in_specs=[SCALAR] + [ALL] * 5,
        out_specs=(ALL,) * 4,
        scratch_shapes=[
            pltpu.VMEM((HALF, HALF), jnp.float32),
            pltpu.VMEM((4, LINE, 128), jnp.float32),
        ],
        compiler_params=PARAMS,
        name="products",
    )(core, grad0, grad1, rows0, rows1, sums)


def fold_kernel(place_ref, own_ref, in1_ref, in2_ref, in3_ref, keep_ref, out1_ref, out2_ref, out3_ref, order_ref):
    place = place_ref[3]
    for d in range(4):
        at = slice(d * QUARTER, (d + 1) * QUARTER)
        block = own_ref[at, :]
        for ref in (in1_ref, in2_ref, in3_ref):
            block += ref[at, :].astype(jnp.float32)
        order_ref[(d - place) & 3] = block
    keep_ref[...] = order_ref[0]
    for by, ref in enumerate((out1_ref, out2_ref, out3_ref)):
        ref[...] = order_ref[by + 1].astype(jnp.bfloat16)


def fold(place, own, terms):
    sent = jax.ShapeDtypeStruct((QUARTER, 128), jnp.bfloat16)
    return pl.pallas_call(
        fold_kernel,
        out_shape=(jax.ShapeDtypeStruct((QUARTER, 128), jnp.float32), sent, sent, sent),
        in_specs=[SCALAR] + [ALL] * 4,
        out_specs=(ALL,) * 4,
        scratch_shapes=[pltpu.VMEM((4, QUARTER, 128), jnp.float32)],
        compiler_params=PARAMS,
        name="fold",
    )(place, own, *terms)


def runs():
    place = column_places()[0]
    found = []
    at = 0
    while at < KIN:
        stop = at + 1
        while stop < KIN and place[stop] == place[stop - 1] + 1 and place[stop] % 128 and stop % 128:
            stop += 1
        found.append((at, int(place[at]), stop - at))
        at = stop
    return found


def finish_kernel(place_ref, *refs):
    *parts, out_ref, norm_ref, held_ref, last_ref = refs
    core, x = place_ref[0], place_ref[4]
    for n, ref in enumerate(parts):
        side, by = divmod(n, 4)
        at = pl.multiple_of(((x - by) & 3) * QUARTER, 16)
        held_ref[core if side == 0 else 1 - core, pl.ds(at, QUARTER), :] = ref[...]
    lane = iota((OWNED, 128), 1)
    for tile in range(pl.cdiv(KIN, 128)):
        acc = None
        for at, src, size in runs():
            if at // 128 != tile:
                continue
            half, column = divmod(src // 128, TILES)
            piece = held_ref[half, column * OWNED : (column + 1) * OWNED, :]
            shift = (at - src) % 128
            if shift:
                piece = pltpu.roll(piece, shift, 1)
            acc = piece if acc is None else jnp.where(lane >= at % 128, piece, acc)
        width = min(128, KIN - tile * 128)
        out_ref[:, tile * 128 : tile * 128 + width] = acc[:, :width]
    last_ref[0:OWNED, :] = held_ref[0, LINE - OWNED :, :] + held_ref[1, LINE - OWNED :, :]
    last_ref[OWNED:, :] = jnp.zeros((384 - OWNED, 128), jnp.float32)
    norm_ref[...] = last_ref[...].T[SUMS : SUMS + 2, :OWNED]


def finish(place, parts):
    return pl.pallas_call(
        finish_kernel,
        out_shape=(
            jax.ShapeDtypeStruct((OWNED, KIN), jnp.float32),
            jax.ShapeDtypeStruct((2, OWNED), jnp.float32),
        ),
        in_specs=[SCALAR] + [ALL] * 8,
        out_specs=(ALL, ALL),
        scratch_shapes=[
            pltpu.VMEM((2, LINE, 128), jnp.float32),
            pltpu.VMEM((384, 128), jnp.float32),
        ],
        compiler_params=PARAMS,
        name="column_order",
    )(place, *parts)


def plane_index(core, x, y):
    return (core * 4 + x) * 4 + y


def plane_shift(by, along_y):
    pairs = []
    for x in range(4):
        for y in range(4):
            for core in range(2):
                to = (x, (y + by) % 4) if core == along_y else ((x + by) % 4, y)
                pairs.append((plane_index(core, x, y), plane_index(core, *to)))
    return pairs


def ring(by):
    return [(i, (i + by) % 4) for i in range(4)]


def copies(array, axis, count):
    array = jnp.broadcast_to(array[None], (count,) + array.shape)
    return lax.all_to_all(array, axis, 0, 0, tiled=True)


def shards(pixels, grad_norm, grad_resid, embed_weight, norm_gain, send_slot, recv_slot):
    plane = ("core", "slab", "fsdp")
    core = lax.axis_index("core").astype(jnp.int32)
    x = lax.axis_index("slab").astype(jnp.int32)
    y = lax.axis_index("fsdp").astype(jnp.int32)
    place = jnp.stack([core, jnp.where(core == 0, y, x), y, jnp.where(core == 0, x, y), x])
    earlier = lax.ppermute(pixels[:, :, 3:4], "slab", ring(1))
    takes = recv_slot.reshape(1, ROWS)
    sends = send_slot.reshape(ROWS, 1)
    packed0 = packed_rows(jnp.ones((1,), jnp.int32), takes, pixels, pixels, 0, 2)
    packed0, shard = lax.optimization_barrier((packed0, embed_weight))
    arrived0 = lax.all_to_all(packed0, ("z", "core"), 0, 0, tiled=True)
    swap = [(0, 1), (1, 0)]
    part = lax.dynamic_slice_in_dim(shard, core * (OWNED // 2), OWNED // 2, 0)
    parts = [lax.ppermute(part, "fsdp", ring(by)) for by in (1, 2, 3)]
    earlier, *parts = lax.optimization_barrier((earlier, *parts))
    packed1 = packed_rows((x > 0).astype(jnp.int32)[None], takes, earlier, pixels, 0, 1)
    arrived1 = lax.all_to_all(packed1, ("z", "core"), 0, 0, tiled=True)
    parts += [lax.ppermute(part, "core", swap) for part in parts]
    weight = padded_weight(place, embed_weight, parts)
    part = first_half(sends, arrived0, weight)
    grads, mine, send, sums = norm_backward(
        place, sends, arrived1, part, weight, grad_norm, grad_resid, norm_gain.reshape(1, D)
    )
    theirs = lax.ppermute(send, "core", swap)
    their_grads = lax.ppermute(grads, "core", swap)
    own, *sent = products(place, grads, their_grads, mine, theirs, sums)
    terms = [lax.ppermute(sent[by - 1], plane, plane_shift(by, 0)) for by in (1, 3, 2)]
    keep, *sent = fold(place, own, terms)
    terms = [lax.ppermute(sent[by - 1], plane, plane_shift(by, 1)) for by in (1, 3, 2)]
    quarter = keep + terms[0].astype(jnp.float32) + terms[1].astype(jnp.float32) + terms[2].astype(jnp.float32)
    quarter = jnp.pad(quarter, ((0, 8 * PIECE - QUARTER), (0, 0)))
    pieces = lax.all_to_all(quarter.reshape(8, PIECE, 128), "z", 0, 0, tiled=True)
    quarter = copies(jnp.sum(pieces, axis=0), "z", 8).reshape(8 * PIECE, 128)[:QUARTER]
    mine = [quarter] + [lax.ppermute(quarter, "slab", ring(by)) for by in (1, 2, 3)]
    return finish(place, mine + [lax.ppermute(part, "core", swap) for part in mine])


def solution(mesh):
    split = Mesh(mesh.devices.reshape(8, 2, 4, 4), ("z", "core", "slab", "fsdp"))
    dp = ("z", "core")
    return jax.shard_map(
        shards,
        mesh=split,
        in_specs=(
            P(dp, "fsdp", "slab", None, None, None),
            P("slab", "fsdp", dp, None),
            P("slab", "fsdp", dp, None),
            P("fsdp", None),
            P(),
            P("slab", "fsdp", dp),
            P("slab", "fsdp", dp),
        ),
        out_specs=(P("fsdp", None), P(None, "fsdp")),
        check_vma=False,
    )
```

```python
import jax
import jax.numpy as jnp
import numpy as np
from jax import lax
from jax.experimental import pallas as pl
from jax.experimental.pallas import tpu as pltpu
from jax.sharding import Mesh
from jax.sharding import PartitionSpec as P

GH = 16
GW = 16
PS = 14
COLOURS = 3
SIDE = 224
ROWS = 512
CAP = 64
PEERS = 16
D = 1280
KIN = 1176
GROUPS = 9
PARTS = COLOURS * PS
FRAME = PARTS * PS
HELD = 296
HALF = 640
TILES = HALF // 128
OWNED = D // 4
LINE = OWNED * TILES
QUARTER = LINE // 4
STEP = 80
PIECE = 56
BLOCK = 256
SUMS = 96
ALL = pl.BlockSpec(memory_space=pltpu.VMEM)
FAR = pl.BlockSpec(memory_space=pltpu.HBM)
SCALAR = pl.BlockSpec(memory_space=pltpu.SMEM)
PARAMS = pltpu.CompilerParams(vmem_limit_bytes=24 * 1024 * 1024)
NORM = pltpu.CompilerParams(vmem_limit_bytes=49 * 1024 * 1024)
WIDE = pltpu.CompilerParams(vmem_limit_bytes=60 * 1024 * 1024)
LANES = (((1,), (1,)), ((), ()))
SUBLANES = (((0,), (0,)), ((), ()))


def one_hot(match):
    return match.astype(jnp.float32).astype(jnp.bfloat16)


def iota(shape, dim):
    return lax.broadcasted_iota(jnp.int32, shape, dim)


def dot(a, b, dims=(((1,), (0,)), ((), ()))):
    return lax.dot_general(a, b, dims, preferred_element_type=jnp.float32)


def column_places():
    place = np.zeros((1, KIN), np.int32)
    for c in range(COLOURS):
        for t in range(2):
            part = c * PS * PS + np.arange(PS * PS)
            at = (c * 2 + t) * PS * PS
            place[0, at : at + PS * PS] = (1 - t) * HALF + part
    return place


def patch_kernel(valid_ref, slot_ref, fa_ref, fb_ref, out_ref, spread_ref, rows_ref):
    src = iota((SIDE, 256), 0)
    place = jnp.where(src >= GROUPS * PS, src + 2, src)
    spread = one_hot(iota((SIDE, 256), 1) == place)
    for k, ref in enumerate((fa_ref, fb_ref)):
        for c in range(COLOURS):
            wide = dot(ref[0, 0, 0, c], spread)
            for h in range(2):
                spread_ref[k, c, h, :SIDE] = wide[:, h * 128 : (h + 1) * 128]

    @pl.when(valid_ref[0] == 0)
    def _():
        spread_ref[0] = jnp.zeros_like(spread_ref[0])

    lane = iota((GH, 128), 1)
    for k in range(2):
        for x in range(GW):
            here = slice((k * GW + x) * GH, (k * GW + x + 1) * GH)
            acc = None
            for n in range(PARTS):
                c, p = divmod(n, PS)
                piece = spread_ref[k, c, x // GROUPS, pl.ds(p, GH, stride=PS), :]
                shift = PS * (n - x % GROUPS) % 128
                if shift:
                    piece = pltpu.roll(piece, shift, 1)
                tile, at = divmod(PS * n, 128)
                acc = piece if acc is None else jnp.where(lane >= at, piece, acc)
                if n == PARTS - 1:
                    acc = jnp.where(lane < at + PS, acc, 0.0)
                if at + PS >= 128 or n == PARTS - 1:
                    rows_ref[here, tile * 128 : (tile + 1) * 128] = acc.astype(jnp.bfloat16)
                    acc = piece
    slots = slot_ref[...]
    kind = iota((16, ROWS), 0)
    digits = jnp.where(kind == 0, slots >> 6, jnp.where(kind == 1, slots & 63, 0))
    dst = iota((ROWS, ROWS), 0)
    order = one_hot(iota((ROWS, ROWS), 1) == (dst & 256) + ((dst & 15) << 4) + ((dst >> 4) & 15))
    digits = dot(order, digits.astype(jnp.float32).astype(jnp.bfloat16), LANES)
    slots = (digits[:, 0:1] * 64.0 + digits[:, 1:2]).astype(jnp.int32)
    side = iota((HELD, 128), 1) < CAP
    for i in range(PEERS // 4):
        pick = one_hot(iota((ROWS, 256), 1) + i * 256 == slots)
        both = dot(rows_ref[...], pick, SUBLANES)
        for j in range(2):
            lo = both[0:HELD, j * 128 : (j + 1) * 128]
            hi = both[HELD : 2 * HELD, j * 128 : (j + 1) * 128]
            peer = i * 4 + j * 2
            out_ref[peer] = jnp.where(side, lo, pltpu.roll(hi, CAP, 1)).astype(jnp.bfloat16)
            out_ref[peer + 1] = jnp.where(side, pltpu.roll(lo, CAP, 1), hi).astype(jnp.bfloat16)


def packed_rows(valid, slots, first, second, first_at, second_at):
    block = (1, 1, 1, COLOURS, SIDE, SIDE)
    shape = (PEERS, HELD, 128)
    return pl.pallas_call(
        patch_kernel,
        out_shape=jax.ShapeDtypeStruct(shape, jnp.bfloat16),
        grid=(1,),
        in_specs=[
            SCALAR,
            pl.BlockSpec((1, ROWS), lambda i: (0, 0)),
            pl.BlockSpec(block, lambda i: (0, 0, first_at, 0, 0, 0)),
            pl.BlockSpec(block, lambda i: (0, 0, second_at, 0, 0, 0)),
        ],
        out_specs=pl.BlockSpec(shape, lambda i: (0, 0, 0)),
        scratch_shapes=[
            pltpu.VMEM((2, COLOURS, 2, GH * (PS + 1), 128), jnp.float32),
            pltpu.VMEM((ROWS, HALF), jnp.bfloat16),
        ],
        compiler_params=WIDE,
        name="patch_rows",
    )(valid, slots, first, second)


def weight_kernel(place_ref, column_ref, own_ref, *refs):
    *parts, out_ref, held_ref = refs
    core, y = place_ref[0], place_ref[2]
    part = OWNED // 2
    held_ref[pl.ds(pl.multiple_of(y * OWNED, 16), OWNED), :] = own_ref[...]
    for n, ref in enumerate(parts):
        side, by = divmod(n, 3)
        row = ((y - by - 1) & 3) * OWNED + (core if side == 0 else 1 - core) * part
        held_ref[pl.ds(pl.multiple_of(row, 16), part), :] = ref[...]
    for i in range(2):
        pick = one_hot(iota((HALF, KIN), 0) + i * HALF == column_ref[...])
        out_ref[:, i * HALF : (i + 1) * HALF] = dot(held_ref[...], pick, LANES).astype(jnp.bfloat16)


def padded_weight(place, own, parts):
    return pl.pallas_call(
        weight_kernel,
        out_shape=jax.ShapeDtypeStruct((D, 2 * HALF), jnp.bfloat16),
        in_specs=[SCALAR] + [ALL] * 8,
        out_specs=ALL,
        scratch_shapes=[pltpu.VMEM((D, KIN), jnp.bfloat16)],
        compiler_params=WIDE,
        name="weight_columns",
    )(place, jnp.asarray(column_places()), own, *parts)


def taken_rows(slot_ref, arr_ref, cols_ref):
    side = iota((HELD, 128), 1) < CAP
    for j in range(PEERS // 2):
        even = arr_ref[2 * j].astype(jnp.float32)
        odd = arr_ref[2 * j + 1].astype(jnp.float32)
        low = jnp.where(side, even, pltpu.roll(odd, CAP, 1))
        high = jnp.where(side, pltpu.roll(even, CAP, 1), odd)
        both = jnp.concatenate([low, high], axis=0).astype(jnp.bfloat16)
        cols_ref[: 2 * HELD, j * 128 : (j + 1) * 128] = both
    cols_ref[2 * HELD :, :] = jnp.zeros((HALF - 2 * HELD, PEERS * CAP), jnp.bfloat16)
    pick = one_hot(iota((ROWS, PEERS * CAP), 1) == slot_ref[...])
    return dot(pick, cols_ref[...], LANES).astype(jnp.bfloat16)


def first_kernel(slot_ref, arr_ref, w_ref, part_ref, cols_ref, rows_ref):
    rows_ref[...] = taken_rows(slot_ref, arr_ref, cols_ref)

    def block(i, carry):
        here = pl.ds(pl.multiple_of(i * 128, 128), 128)
        part_ref[here, :D] = dot(rows_ref[here, :], w_ref[:, :HALF], LANES)
        part_ref[here, D:] = rows_ref[here, :].astype(jnp.float32)
        return carry

    lax.fori_loop(0, ROWS // 128, block, 0)


def first_half(slots, arrived, weight):
    return pl.pallas_call(
        first_kernel,
        out_shape=jax.ShapeDtypeStruct((ROWS, D + HALF), jnp.float32),
        in_specs=[ALL] * 3,
        out_specs=ALL,
        scratch_shapes=[
            pltpu.VMEM((HALF, PEERS * CAP), jnp.bfloat16),
            pltpu.VMEM((ROWS, HALF), jnp.bfloat16),
        ],
        compiler_params=WIDE,
        name="first_half",
    )(slots, arrived, weight)


def backward_kernel(core_ref, slot_ref, arr_ref, part_far, w_far, g_far, r_far, gain_ref, grad_ref, mine_ref, send_ref, sums_ref, cols_ref, rows1_ref, part_ref, w_ref, g_ref, r_ref, sems):
    reads = [
        pltpu.make_async_copy(w_far.at[:, HALF:], w_ref, sems.at[0]),
        pltpu.make_async_copy(part_far, part_ref, sems.at[1]),
        pltpu.make_async_copy(g_far.at[0, 0], g_ref, sems.at[2]),
        pltpu.make_async_copy(r_far.at[0, 0], r_ref, sems.at[3]),
    ]
    for read in reads:
        read.start()
    rows1_ref[...] = taken_rows(slot_ref, arr_ref, cols_ref)
    for read in reads:
        read.wait()

    @pl.when(core_ref[0] == 0)
    def _():
        mine_ref[...] = part_ref[:, D:].astype(jnp.bfloat16)
        send_ref[...] = rows1_ref[...]

    @pl.when(core_ref[0] != 0)
    def _():
        mine_ref[...] = rows1_ref[...]
        send_ref[...] = part_ref[:, D:].astype(jnp.bfloat16)

    sums_ref[...] = jnp.zeros_like(sums_ref)
    for i in range(D // 256):
        at = slice(i * 256, (i + 1) * 256)
        part_ref[:, at] += dot(rows1_ref[...], w_ref[at, :], LANES)

    def block(i, carry):
        here = pl.ds(pl.multiple_of(i * BLOCK, BLOCK), BLOCK)
        embedded = part_ref[here, :D]
        deviation = embedded - jnp.mean(embedded, axis=-1, keepdims=True)
        variance = jnp.mean(deviation * deviation, axis=-1, keepdims=True)
        inverse_std = lax.rsqrt(variance + 1e-06)
        normalized = deviation * inverse_std
        upstream_norm = g_ref[here, :].astype(jnp.float32)
        upstream = upstream_norm * gain_ref[...]
        inner = jnp.mean(upstream * normalized, axis=-1, keepdims=True)
        level = jnp.mean(upstream, axis=-1, keepdims=True)
        input_grad = r_ref[here, :].astype(jnp.float32) + inverse_std * (
            upstream - level - normalized * inner
        )
        grad_ref[here, :] = input_grad.astype(jnp.bfloat16)
        sums_ref[0:8, :] += jnp.sum((upstream_norm * normalized).reshape(BLOCK // 8, 8, D), axis=0)
        sums_ref[8:16, :] += jnp.sum(upstream_norm.reshape(BLOCK // 8, 8, D), axis=0)
        return carry

    lax.fori_loop(0, ROWS // BLOCK, block, 0)


def norm_backward(core, slots, arrived, part, weight, grad_norm, grad_resid, gain):
    half = jax.ShapeDtypeStruct((ROWS, HALF), jnp.bfloat16)
    return pl.pallas_call(
        backward_kernel,
        out_shape=(
            jax.ShapeDtypeStruct((ROWS, D), jnp.bfloat16),
            half,
            half,
            jax.ShapeDtypeStruct((16, D), jnp.float32),
        ),
        in_specs=[SCALAR, ALL, ALL, FAR, FAR, FAR, FAR, ALL],
        out_specs=(ALL,) * 4,
        scratch_shapes=[
            pltpu.VMEM((HALF, PEERS * CAP), jnp.bfloat16),
            pltpu.VMEM((ROWS, HALF), jnp.bfloat16),
            pltpu.VMEM((ROWS, D + HALF), jnp.float32),
            pltpu.VMEM((D, HALF), jnp.bfloat16),
            pltpu.VMEM((ROWS, D), jnp.bfloat16),
            pltpu.VMEM((ROWS, D), jnp.bfloat16),
            pltpu.SemaphoreType.DMA((4,)),
        ],
        compiler_params=NORM,
        name="norm_backward",
    )(core, slots, arrived, part, weight, grad_norm, grad_resid, gain)


def own_kernel(grad_ref, rows_ref, sums_ref, out_ref):
    kind = iota((128, HALF), 0)
    for i in range(D // HALF):
        here = slice(i * HALF, (i + 1) * HALF)
        out_ref[here, :] = dot(grad_ref[:, here], rows_ref[...], SUBLANES)
        gain_sum = jnp.sum(sums_ref[0:8, here], axis=0, keepdims=True)
        bias_sum = jnp.sum(sums_ref[8:16, here], axis=0, keepdims=True)
        sums = jnp.where(kind == SUMS, gain_sum, jnp.where(kind == SUMS + 1, bias_sum, 0.0))
        out_ref[here, HALF - 128 :] += sums.T


def own_products(grad, rows, sums):
    return pl.pallas_call(
        own_kernel,
        out_shape=jax.ShapeDtypeStruct((D, HALF), jnp.float32),
        in_specs=[ALL] * 3,
        out_specs=ALL,
        compiler_params=PARAMS,
        cost_estimate=pl.CostEstimate(flops=2 * ROWS * D * HALF, bytes_accessed=6 * 1024 * 1024, transcendentals=0),
        name="own_products",
    )(grad, rows, sums)


def product_kernel(core_ref, part_ref, grad_ref, rows_ref, own_ref, out1_ref, out2_ref, out3_ref, terms_ref, order_ref):
    core, place = core_ref[0], core_ref[1]
    for i in range(D // HALF):
        here = slice(i * HALF, (i + 1) * HALF)
        terms_ref[...] = part_ref[here, :] + dot(grad_ref[:, here], rows_ref[...], SUBLANES)
        for n in range(HALF // STEP):
            y, r = divmod(i * (HALF // STEP) + n, OWNED // STEP)
            for t in range(TILES):
                o = t * (OWNED // STEP) + r
                block = terms_ref[n * STEP : (n + 1) * STEP, t * 128 : (t + 1) * 128]
                to = jnp.where(core == 0, y, o // 5)
                at = jnp.where(core == 0, o * STEP, y * QUARTER + o % 5 * STEP)
                at = pl.ds(pl.multiple_of(at, 16), STEP)
                order_ref[(to - place) & 3, at, :] = block
    own_ref[...] = order_ref[0]
    for by, ref in enumerate((out1_ref, out2_ref, out3_ref)):
        ref[...] = order_ref[by + 1].astype(jnp.bfloat16)


def products(core, part, grad, rows):
    sent = jax.ShapeDtypeStruct((LINE, 128), jnp.bfloat16)
    return pl.pallas_call(
        product_kernel,
        out_shape=(jax.ShapeDtypeStruct((LINE, 128), jnp.float32), sent, sent, sent),
        in_specs=[SCALAR] + [ALL] * 3,
        out_specs=(ALL,) * 4,
        scratch_shapes=[
            pltpu.VMEM((HALF, HALF), jnp.float32),
            pltpu.VMEM((4, LINE, 128), jnp.float32),
        ],
        compiler_params=PARAMS,
        name="products",
    )(core, part, grad, rows)


def fold_kernel(place_ref, own_ref, in1_ref, in2_ref, in3_ref, keep_ref, out1_ref, out2_ref, out3_ref, order_ref):
    place = place_ref[3]
    for d in range(4):
        at = slice(d * QUARTER, (d + 1) * QUARTER)
        block = own_ref[at, :]
        for ref in (in1_ref, in2_ref, in3_ref):
            block += ref[at, :].astype(jnp.float32)
        order_ref[(d - place) & 3] = block
    keep_ref[...] = order_ref[0]
    for by, ref in enumerate((out1_ref, out2_ref, out3_ref)):
        ref[...] = order_ref[by + 1].astype(jnp.bfloat16)


def fold(place, own, terms):
    sent = jax.ShapeDtypeStruct((QUARTER, 128), jnp.bfloat16)
    return pl.pallas_call(
        fold_kernel,
        out_shape=(jax.ShapeDtypeStruct((QUARTER, 128), jnp.float32), sent, sent, sent),
        in_specs=[SCALAR] + [ALL] * 4,
        out_specs=(ALL,) * 4,
        scratch_shapes=[pltpu.VMEM((4, QUARTER, 128), jnp.float32)],
        compiler_params=PARAMS,
        name="fold",
    )(place, own, *terms)


def runs():
    place = column_places()[0]
    found = []
    at = 0
    while at < KIN:
        stop = at + 1
        while stop < KIN and place[stop] == place[stop - 1] + 1 and place[stop] % 128 and stop % 128:
            stop += 1
        found.append((at, int(place[at]), stop - at))
        at = stop
    return found


def finish_kernel(place_ref, *refs):
    *parts, out_ref, norm_ref, held_ref, last_ref = refs
    core, x = place_ref[0], place_ref[4]
    for n, ref in enumerate(parts):
        side, by = divmod(n, 4)
        at = pl.multiple_of(((x - by) & 3) * QUARTER, 16)
        held_ref[core if side == 0 else 1 - core, pl.ds(at, QUARTER), :] = ref[...]
    lane = iota((OWNED, 128), 1)
    for tile in range(pl.cdiv(KIN, 128)):
        acc = None
        for at, src, size in runs():
            if at // 128 != tile:
                continue
            half, column = divmod(src // 128, TILES)
            piece = held_ref[half, column * OWNED : (column + 1) * OWNED, :]
            shift = (at - src) % 128
            if shift:
                piece = pltpu.roll(piece, shift, 1)
            acc = piece if acc is None else jnp.where(lane >= at % 128, piece, acc)
        width = min(128, KIN - tile * 128)
        out_ref[:, tile * 128 : tile * 128 + width] = acc[:, :width]
    last_ref[0:OWNED, :] = held_ref[0, LINE - OWNED :, :] + held_ref[1, LINE - OWNED :, :]
    last_ref[OWNED:, :] = jnp.zeros((384 - OWNED, 128), jnp.float32)
    norm_ref[...] = last_ref[...].T[SUMS : SUMS + 2, :OWNED]


def finish(place, parts):
    return pl.pallas_call(
        finish_kernel,
        out_shape=(
            jax.ShapeDtypeStruct((OWNED, KIN), jnp.float32),
            jax.ShapeDtypeStruct((2, OWNED), jnp.float32),
        ),
        in_specs=[SCALAR] + [ALL] * 8,
        out_specs=(ALL, ALL),
        scratch_shapes=[
            pltpu.VMEM((2, LINE, 128), jnp.float32),
            pltpu.VMEM((384, 128), jnp.float32),
        ],
        compiler_params=PARAMS,
        name="column_order",
    )(place, *parts)


def plane_index(core, x, y):
    return (core * 4 + x) * 4 + y


def plane_shift(by, along_y):
    pairs = []
    for x in range(4):
        for y in range(4):
            for core in range(2):
                to = (x, (y + by) % 4) if core == along_y else ((x + by) % 4, y)
                pairs.append((plane_index(core, x, y), plane_index(core, *to)))
    return pairs


def ring(by):
    return [(i, (i + by) % 4) for i in range(4)]


def copies(array, axis, count):
    array = jnp.broadcast_to(array[None], (count,) + array.shape)
    return lax.all_to_all(array, axis, 0, 0, tiled=True)


def shards(pixels, grad_norm, grad_resid, embed_weight, norm_gain, send_slot, recv_slot):
    plane = ("core", "slab", "fsdp")
    core = lax.axis_index("core").astype(jnp.int32)
    x = lax.axis_index("slab").astype(jnp.int32)
    y = lax.axis_index("fsdp").astype(jnp.int32)
    place = jnp.stack([core, jnp.where(core == 0, y, x), y, jnp.where(core == 0, x, y), x])
    earlier = lax.ppermute(pixels[:, :, 3:4], "slab", ring(1))
    takes = recv_slot.reshape(1, ROWS)
    sends = send_slot.reshape(ROWS, 1)
    packed0 = packed_rows(jnp.ones((1,), jnp.int32), takes, pixels, pixels, 0, 2)
    packed0, shard = lax.optimization_barrier((packed0, embed_weight))
    arrived0 = lax.all_to_all(packed0, ("z", "core"), 0, 0, tiled=True)
    swap = [(0, 1), (1, 0)]
    part = lax.dynamic_slice_in_dim(shard, core * (OWNED // 2), OWNED // 2, 0)
    parts = [lax.ppermute(part, "fsdp", ring(by)) for by in (1, 2, 3)]
    earlier, *parts = lax.optimization_barrier((earlier, *parts))
    packed1 = packed_rows((x > 0).astype(jnp.int32)[None], takes, earlier, pixels, 0, 1)
    arrived1 = lax.all_to_all(packed1, ("z", "core"), 0, 0, tiled=True)
    parts += [lax.ppermute(part, "core", swap) for part in parts]
    weight = padded_weight(place, embed_weight, parts)
    part = first_half(sends, arrived0, weight)
    grads, mine, send, sums = norm_backward(
        place, sends, arrived1, part, weight, grad_norm, grad_resid, norm_gain.reshape(1, D)
    )
    theirs = lax.ppermute(send, "core", swap)
    their_grads = lax.ppermute(grads, "core", swap)
    own, *sent = products(place, own_products(grads, mine, sums), their_grads, theirs)
    terms = [lax.ppermute(sent[by - 1], plane, plane_shift(by, 0)) for by in (1, 3, 2)]
    keep, *sent = fold(place, own, terms)
    terms = [lax.ppermute(sent[by - 1], plane, plane_shift(by, 1)) for by in (1, 3, 2)]
    quarter = keep + terms[0].astype(jnp.float32) + terms[1].astype(jnp.float32) + terms[2].astype(jnp.float32)
    quarter = jnp.pad(quarter, ((0, 8 * PIECE - QUARTER), (0, 0)))
    pieces = lax.all_to_all(quarter.reshape(8, PIECE, 128), "z", 0, 0, tiled=True)
    quarter = copies(jnp.sum(pieces, axis=0), "z", 8).reshape(8 * PIECE, 128)[:QUARTER]
    mine = [quarter] + [lax.ppermute(quarter, "slab", ring(by)) for by in (1, 2, 3)]
    return finish(place, mine + [lax.ppermute(part, "core", swap) for part in mine])


def solution(mesh):
    split = Mesh(mesh.devices.reshape(8, 2, 4, 4), ("z", "core", "slab", "fsdp"))
    dp = ("z", "core")
    return jax.shard_map(
        shards,
        mesh=split,
        in_specs=(
            P(dp, "fsdp", "slab", None, None, None),
            P("slab", "fsdp", dp, None),
            P("slab", "fsdp", dp, None),
            P("fsdp", None),
            P(),
            P("slab", "fsdp", dp),
            P("slab", "fsdp", dp),
        ),
        out_specs=(P("fsdp", None), P(None, "fsdp")),
        check_vma=False,
    )
```

```python
import jax
import jax.numpy as jnp
import numpy as np
from jax import lax
from jax.experimental import pallas as pl
from jax.experimental.pallas import tpu as pltpu
from jax.sharding import Mesh
from jax.sharding import PartitionSpec as P

GH = 16
GW = 16
PS = 14
COLOURS = 3
SIDE = 224
ROWS = 512
CAP = 64
PEERS = 16
D = 1280
KIN = 1176
GROUPS = 9
PARTS = COLOURS * PS
FRAME = PARTS * PS
HELD = 296
HALF = 640
TILES = HALF // 128
OWNED = D // 4
LINE = OWNED * TILES
QUARTER = LINE // 4
STEP = 80
PIECE = 56
BLOCK = 512
SUMS = 96
ALL = pl.BlockSpec(memory_space=pltpu.VMEM)
FAR = pl.BlockSpec(memory_space=pltpu.HBM)
SCALAR = pl.BlockSpec(memory_space=pltpu.SMEM)
PARAMS = pltpu.CompilerParams(vmem_limit_bytes=24 * 1024 * 1024)
NORM = pltpu.CompilerParams(vmem_limit_bytes=49 * 1024 * 1024)
WIDE = pltpu.CompilerParams(vmem_limit_bytes=60 * 1024 * 1024)
LANES = (((1,), (1,)), ((), ()))
SUBLANES = (((0,), (0,)), ((), ()))


def one_hot(match):
    return match.astype(jnp.float32).astype(jnp.bfloat16)


def iota(shape, dim):
    return lax.broadcasted_iota(jnp.int32, shape, dim)


def dot(a, b, dims=(((1,), (0,)), ((), ()))):
    return lax.dot_general(a, b, dims, preferred_element_type=jnp.float32)


def column_places():
    place = np.zeros((1, KIN), np.int32)
    for c in range(COLOURS):
        for t in range(2):
            part = c * PS * PS + np.arange(PS * PS)
            at = (c * 2 + t) * PS * PS
            place[0, at : at + PS * PS] = (1 - t) * HALF + part
    return place


def patch_kernel(valid_ref, slot_ref, fa_ref, fb_ref, out_ref, spread_ref, rows_ref):
    src = iota((SIDE, 256), 0)
    place = jnp.where(src >= GROUPS * PS, src + 2, src)
    spread = one_hot(iota((SIDE, 256), 1) == place)
    for k, ref in enumerate((fa_ref, fb_ref)):
        for c in range(COLOURS):
            wide = dot(ref[0, 0, 0, c], spread)
            for h in range(2):
                spread_ref[k, c, h, :SIDE] = wide[:, h * 128 : (h + 1) * 128]

    @pl.when(valid_ref[0] == 0)
    def _():
        spread_ref[0] = jnp.zeros_like(spread_ref[0])

    lane = iota((GH, 128), 1)
    for k in range(2):
        for x in range(GW):
            here = slice((k * GW + x) * GH, (k * GW + x + 1) * GH)
            acc = None
            for n in range(PARTS):
                c, p = divmod(n, PS)
                piece = spread_ref[k, c, x // GROUPS, pl.ds(p, GH, stride=PS), :]
                shift = PS * (n - x % GROUPS) % 128
                if shift:
                    piece = pltpu.roll(piece, shift, 1)
                tile, at = divmod(PS * n, 128)
                acc = piece if acc is None else jnp.where(lane >= at, piece, acc)
                if n == PARTS - 1:
                    acc = jnp.where(lane < at + PS, acc, 0.0)
                if at + PS >= 128 or n == PARTS - 1:
                    rows_ref[here, tile * 128 : (tile + 1) * 128] = acc.astype(jnp.bfloat16)
                    acc = piece
    slots = slot_ref[...]
    kind = iota((16, ROWS), 0)
    digits = jnp.where(kind == 0, slots >> 6, jnp.where(kind == 1, slots & 63, 0))
    dst = iota((ROWS, ROWS), 0)
    order = one_hot(iota((ROWS, ROWS), 1) == (dst & 256) + ((dst & 15) << 4) + ((dst >> 4) & 15))
    digits = dot(order, digits.astype(jnp.float32).astype(jnp.bfloat16), LANES)
    slots = (digits[:, 0:1] * 64.0 + digits[:, 1:2]).astype(jnp.int32)
    side = iota((HELD, 128), 1) < CAP
    for i in range(PEERS // 4):
        pick = one_hot(iota((ROWS, 256), 1) + i * 256 == slots)
        both = dot(rows_ref[...], pick, SUBLANES)
        for j in range(2):
            lo = both[0:HELD, j * 128 : (j + 1) * 128]
            hi = both[HELD : 2 * HELD, j * 128 : (j + 1) * 128]
            peer = i * 4 + j * 2
            out_ref[peer] = jnp.where(side, lo, pltpu.roll(hi, CAP, 1)).astype(jnp.bfloat16)
            out_ref[peer + 1] = jnp.where(side, pltpu.roll(lo, CAP, 1), hi).astype(jnp.bfloat16)


def packed_rows(valid, slots, first, second, first_at, second_at):
    block = (1, 1, 1, COLOURS, SIDE, SIDE)
    shape = (PEERS, HELD, 128)
    return pl.pallas_call(
        patch_kernel,
        out_shape=jax.ShapeDtypeStruct(shape, jnp.bfloat16),
        grid=(1,),
        in_specs=[
            SCALAR,
            pl.BlockSpec((1, ROWS), lambda i: (0, 0)),
            pl.BlockSpec(block, lambda i: (0, 0, first_at, 0, 0, 0)),
            pl.BlockSpec(block, lambda i: (0, 0, second_at, 0, 0, 0)),
        ],
        out_specs=pl.BlockSpec(shape, lambda i: (0, 0, 0)),
        scratch_shapes=[
            pltpu.VMEM((2, COLOURS, 2, GH * (PS + 1), 128), jnp.float32),
            pltpu.VMEM((ROWS, HALF), jnp.bfloat16),
        ],
        compiler_params=WIDE,
        name="patch_rows",
    )(valid, slots, first, second)


def weight_kernel(place_ref, column_ref, own_ref, *refs):
    *parts, out_ref, held_ref = refs
    core, y = place_ref[0], place_ref[2]
    part = OWNED // 2
    held_ref[pl.ds(pl.multiple_of(y * OWNED, 16), OWNED), :] = own_ref[...]
    for n, ref in enumerate(parts):
        side, by = divmod(n, 3)
        row = ((y - by - 1) & 3) * OWNED + (core if side == 0 else 1 - core) * part
        held_ref[pl.ds(pl.multiple_of(row, 16), part), :] = ref[...]
    for i in range(2):
        pick = one_hot(iota((HALF, KIN), 0) + i * HALF == column_ref[...])
        out_ref[:, i * HALF : (i + 1) * HALF] = dot(held_ref[...], pick, LANES).astype(jnp.bfloat16)


def padded_weight(place, own, parts):
    return pl.pallas_call(
        weight_kernel,
        out_shape=jax.ShapeDtypeStruct((D, 2 * HALF), jnp.bfloat16),
        in_specs=[SCALAR] + [ALL] * 8,
        out_specs=ALL,
        scratch_shapes=[pltpu.VMEM((D, KIN), jnp.bfloat16)],
        compiler_params=WIDE,
        name="weight_columns",
    )(place, jnp.asarray(column_places()), own, *parts)


def taken_rows(slot_ref, arr_ref, cols_ref):
    side = iota((HELD, 128), 1) < CAP
    for j in range(PEERS // 2):
        even = arr_ref[2 * j].astype(jnp.float32)
        odd = arr_ref[2 * j + 1].astype(jnp.float32)
        low = jnp.where(side, even, pltpu.roll(odd, CAP, 1))
        high = jnp.where(side, pltpu.roll(even, CAP, 1), odd)
        both = jnp.concatenate([low, high], axis=0).astype(jnp.bfloat16)
        cols_ref[: 2 * HELD, j * 128 : (j + 1) * 128] = both
    cols_ref[2 * HELD :, :] = jnp.zeros((HALF - 2 * HELD, PEERS * CAP), jnp.bfloat16)
    pick = one_hot(iota((ROWS, PEERS * CAP), 1) == slot_ref[...])
    return dot(pick, cols_ref[...], LANES).astype(jnp.bfloat16)


def first_kernel(slot_ref, arr_ref, w_ref, part_ref, cols_ref, rows_ref):
    rows_ref[...] = taken_rows(slot_ref, arr_ref, cols_ref)

    def block(i, carry):
        here = pl.ds(pl.multiple_of(i * 128, 128), 128)
        part_ref[here, :D] = dot(rows_ref[here, :], w_ref[:, :HALF], LANES)
        part_ref[here, D:] = rows_ref[here, :].astype(jnp.float32)
        return carry

    lax.fori_loop(0, ROWS // 128, block, 0)


def first_half(slots, arrived, weight):
    return pl.pallas_call(
        first_kernel,
        out_shape=jax.ShapeDtypeStruct((ROWS, D + HALF), jnp.float32),
        in_specs=[ALL] * 3,
        out_specs=ALL,
        scratch_shapes=[
            pltpu.VMEM((HALF, PEERS * CAP), jnp.bfloat16),
            pltpu.VMEM((ROWS, HALF), jnp.bfloat16),
        ],
        compiler_params=WIDE,
        name="first_half",
    )(slots, arrived, weight)


def backward_kernel(core_ref, slot_ref, arr_ref, part_far, w_far, g_far, r_far, gain_ref, grad_ref, mine_ref, send_ref, sums_ref, cols_ref, rows1_ref, part_ref, w_ref, g_ref, r_ref, sems):
    reads = [
        pltpu.make_async_copy(w_far.at[:, HALF:], w_ref, sems.at[0]),
        pltpu.make_async_copy(part_far, part_ref, sems.at[1]),
        pltpu.make_async_copy(g_far.at[0, 0], g_ref, sems.at[2]),
        pltpu.make_async_copy(r_far.at[0, 0], r_ref, sems.at[3]),
    ]
    for read in reads:
        read.start()
    rows1_ref[...] = taken_rows(slot_ref, arr_ref, cols_ref)
    for read in reads:
        read.wait()

    @pl.when(core_ref[0] == 0)
    def _():
        mine_ref[...] = part_ref[:, D:].astype(jnp.bfloat16)
        send_ref[...] = rows1_ref[...]

    @pl.when(core_ref[0] != 0)
    def _():
        mine_ref[...] = rows1_ref[...]
        send_ref[...] = part_ref[:, D:].astype(jnp.bfloat16)

    sums_ref[...] = jnp.zeros_like(sums_ref)
    for i in range(D // 256):
        at = slice(i * 256, (i + 1) * 256)
        part_ref[:, at] += dot(rows1_ref[...], w_ref[at, :], LANES)

    def block(i, carry):
        here = pl.ds(pl.multiple_of(i * BLOCK, BLOCK), BLOCK)
        embedded = part_ref[here, :D]
        deviation = embedded - jnp.mean(embedded, axis=-1, keepdims=True)
        variance = jnp.mean(deviation * deviation, axis=-1, keepdims=True)
        inverse_std = lax.rsqrt(variance + 1e-06)
        normalized = deviation * inverse_std
        upstream_norm = g_ref[here, :].astype(jnp.float32)
        upstream = upstream_norm * gain_ref[...]
        inner = jnp.mean(upstream * normalized, axis=-1, keepdims=True)
        level = jnp.mean(upstream, axis=-1, keepdims=True)
        input_grad = r_ref[here, :].astype(jnp.float32) + inverse_std * (
            upstream - level - normalized * inner
        )
        grad_ref[here, :] = input_grad.astype(jnp.bfloat16)
        sums_ref[0:8, :] += jnp.sum((upstream_norm * normalized).reshape(BLOCK // 8, 8, D), axis=0)
        sums_ref[8:16, :] += jnp.sum(upstream_norm.reshape(BLOCK // 8, 8, D), axis=0)
        return carry

    lax.fori_loop(0, ROWS // BLOCK, block, 0)


def norm_backward(core, slots, arrived, part, weight, grad_norm, grad_resid, gain):
    half = jax.ShapeDtypeStruct((ROWS, HALF), jnp.bfloat16)
    return pl.pallas_call(
        backward_kernel,
        out_shape=(
            jax.ShapeDtypeStruct((ROWS, D), jnp.bfloat16),
            half,
            half,
            jax.ShapeDtypeStruct((16, D), jnp.float32),
        ),
        in_specs=[SCALAR, ALL, ALL, FAR, FAR, FAR, FAR, ALL],
        out_specs=(ALL,) * 4,
        scratch_shapes=[
            pltpu.VMEM((HALF, PEERS * CAP), jnp.bfloat16),
            pltpu.VMEM((ROWS, HALF), jnp.bfloat16),
            pltpu.VMEM((ROWS, D + HALF), jnp.float32),
            pltpu.VMEM((D, HALF), jnp.bfloat16),
            pltpu.VMEM((ROWS, D), jnp.bfloat16),
            pltpu.VMEM((ROWS, D), jnp.bfloat16),
            pltpu.SemaphoreType.DMA((4,)),
        ],
        compiler_params=NORM,
        name="norm_backward",
    )(core, slots, arrived, part, weight, grad_norm, grad_resid, gain)


def own_kernel(grad_ref, rows_ref, sums_ref, out_ref):
    kind = iota((128, HALF), 0)
    for i in range(D // HALF):
        here = slice(i * HALF, (i + 1) * HALF)
        out_ref[here, :] = dot(grad_ref[:, here], rows_ref[...], SUBLANES)
        gain_sum = jnp.sum(sums_ref[0:8, here], axis=0, keepdims=True)
        bias_sum = jnp.sum(sums_ref[8:16, here], axis=0, keepdims=True)
        sums = jnp.where(kind == SUMS, gain_sum, jnp.where(kind == SUMS + 1, bias_sum, 0.0))
        out_ref[here, HALF - 128 :] += sums.T


def own_products(grad, rows, sums):
    return pl.pallas_call(
        own_kernel,
        out_shape=jax.ShapeDtypeStruct((D, HALF), jnp.float32),
        in_specs=[ALL] * 3,
        out_specs=ALL,
        compiler_params=PARAMS,
        cost_estimate=pl.CostEstimate(flops=2 * ROWS * D * HALF, bytes_accessed=6 * 1024 * 1024, transcendentals=0),
        name="own_products",
    )(grad, rows, sums)


def product_kernel(core_ref, part_ref, grad_ref, rows_ref, own_ref, out1_ref, out2_ref, out3_ref, terms_ref, order_ref):
    core, place = core_ref[0], core_ref[1]
    for i in range(D // HALF):
        here = slice(i * HALF, (i + 1) * HALF)
        terms_ref[...] = part_ref[here, :] + dot(grad_ref[:, here], rows_ref[...], SUBLANES)
        for n in range(HALF // STEP):
            y, r = divmod(i * (HALF // STEP) + n, OWNED // STEP)
            for t in range(TILES):
                o = t * (OWNED // STEP) + r
                block = terms_ref[n * STEP : (n + 1) * STEP, t * 128 : (t + 1) * 128]
                to = jnp.where(core == 0, y, o // 5)
                at = jnp.where(core == 0, o * STEP, y * QUARTER + o % 5 * STEP)
                at = pl.ds(pl.multiple_of(at, 16), STEP)
                order_ref[(to - place) & 3, at, :] = block
    own_ref[...] = order_ref[0]
    for by, ref in enumerate((out1_ref, out2_ref, out3_ref)):
        ref[...] = order_ref[by + 1].astype(jnp.bfloat16)


def products(core, part, grad, rows):
    sent = jax.ShapeDtypeStruct((LINE, 128), jnp.bfloat16)
    return pl.pallas_call(
        product_kernel,
        out_shape=(jax.ShapeDtypeStruct((LINE, 128), jnp.float32), sent, sent, sent),
        in_specs=[SCALAR] + [ALL] * 3,
        out_specs=(ALL,) * 4,
        scratch_shapes=[
            pltpu.VMEM((HALF, HALF), jnp.float32),
            pltpu.VMEM((4, LINE, 128), jnp.float32),
        ],
        compiler_params=PARAMS,
        name="products",
    )(core, part, grad, rows)


def fold_kernel(place_ref, own_ref, in1_ref, in2_ref, in3_ref, keep_ref, out1_ref, out2_ref, out3_ref, order_ref):
    place = place_ref[3]
    for d in range(4):
        at = slice(d * QUARTER, (d + 1) * QUARTER)
        block = own_ref[at, :]
        for ref in (in1_ref, in2_ref, in3_ref):
            block += ref[at, :].astype(jnp.float32)
        order_ref[(d - place) & 3] = block
    keep_ref[...] = order_ref[0]
    for by, ref in enumerate((out1_ref, out2_ref, out3_ref)):
        ref[...] = order_ref[by + 1].astype(jnp.bfloat16)


def fold(place, own, terms):
    sent = jax.ShapeDtypeStruct((QUARTER, 128), jnp.bfloat16)
    return pl.pallas_call(
        fold_kernel,
        out_shape=(jax.ShapeDtypeStruct((QUARTER, 128), jnp.float32), sent, sent, sent),
        in_specs=[SCALAR] + [ALL] * 4,
        out_specs=(ALL,) * 4,
        scratch_shapes=[pltpu.VMEM((4, QUARTER, 128), jnp.float32)],
        compiler_params=PARAMS,
        name="fold",
    )(place, own, *terms)


def runs():
    place = column_places()[0]
    found = []
    at = 0
    while at < KIN:
        stop = at + 1
        while stop < KIN and place[stop] == place[stop - 1] + 1 and place[stop] % 128 and stop % 128:
            stop += 1
        found.append((at, int(place[at]), stop - at))
        at = stop
    return found


def finish_kernel(place_ref, *refs):
    *parts, out_ref, norm_ref, held_ref, last_ref = refs
    core, x = place_ref[0], place_ref[4]
    for n, ref in enumerate(parts):
        side, by = divmod(n, 4)
        at = pl.multiple_of(((x - by) & 3) * QUARTER, 16)
        held_ref[core if side == 0 else 1 - core, pl.ds(at, QUARTER), :] = ref[...]
    lane = iota((OWNED, 128), 1)
    for tile in range(pl.cdiv(KIN, 128)):
        acc = None
        for at, src, size in runs():
            if at // 128 != tile:
                continue
            half, column = divmod(src // 128, TILES)
            piece = held_ref[half, column * OWNED : (column + 1) * OWNED, :]
            shift = (at - src) % 128
            if shift:
                piece = pltpu.roll(piece, shift, 1)
            acc = piece if acc is None else jnp.where(lane >= at % 128, piece, acc)
        width = min(128, KIN - tile * 128)
        out_ref[:, tile * 128 : tile * 128 + width] = acc[:, :width]
    last_ref[0:OWNED, :] = held_ref[0, LINE - OWNED :, :] + held_ref[1, LINE - OWNED :, :]
    last_ref[OWNED:, :] = jnp.zeros((384 - OWNED, 128), jnp.float32)
    norm_ref[...] = last_ref[...].T[SUMS : SUMS + 2, :OWNED]


def finish(place, parts):
    return pl.pallas_call(
        finish_kernel,
        out_shape=(
            jax.ShapeDtypeStruct((OWNED, KIN), jnp.float32),
            jax.ShapeDtypeStruct((2, OWNED), jnp.float32),
        ),
        in_specs=[SCALAR] + [ALL] * 8,
        out_specs=(ALL, ALL),
        scratch_shapes=[
            pltpu.VMEM((2, LINE, 128), jnp.float32),
            pltpu.VMEM((384, 128), jnp.float32),
        ],
        compiler_params=PARAMS,
        name="column_order",
    )(place, *parts)


def plane_index(core, x, y):
    return (core * 4 + x) * 4 + y


def plane_shift(by, along_y):
    pairs = []
    for x in range(4):
        for y in range(4):
            for core in range(2):
                to = (x, (y + by) % 4) if core == along_y else ((x + by) % 4, y)
                pairs.append((plane_index(core, x, y), plane_index(core, *to)))
    return pairs


def ring(by):
    return [(i, (i + by) % 4) for i in range(4)]


def copies(array, axis, count):
    array = jnp.broadcast_to(array[None], (count,) + array.shape)
    return lax.all_to_all(array, axis, 0, 0, tiled=True)


def shards(pixels, grad_norm, grad_resid, embed_weight, norm_gain, send_slot, recv_slot):
    plane = ("core", "slab", "fsdp")
    core = lax.axis_index("core").astype(jnp.int32)
    x = lax.axis_index("slab").astype(jnp.int32)
    y = lax.axis_index("fsdp").astype(jnp.int32)
    place = jnp.stack([core, jnp.where(core == 0, y, x), y, jnp.where(core == 0, x, y), x])
    earlier = lax.ppermute(pixels[:, :, 3:4], "slab", ring(1))
    takes = recv_slot.reshape(1, ROWS)
    sends = send_slot.reshape(ROWS, 1)
    packed0 = packed_rows(jnp.ones((1,), jnp.int32), takes, pixels, pixels, 0, 2)
    packed0, shard = lax.optimization_barrier((packed0, embed_weight))
    arrived0 = lax.all_to_all(packed0, ("z", "core"), 0, 0, tiled=True)
    swap = [(0, 1), (1, 0)]
    part = lax.dynamic_slice_in_dim(shard, core * (OWNED // 2), OWNED // 2, 0)
    parts = [lax.ppermute(part, "fsdp", ring(by)) for by in (1, 2, 3)]
    earlier, *parts = lax.optimization_barrier((earlier, *parts))
    packed1 = packed_rows((x > 0).astype(jnp.int32)[None], takes, earlier, pixels, 0, 1)
    arrived1 = lax.all_to_all(packed1, ("z", "core"), 0, 0, tiled=True)
    parts += [lax.ppermute(part, "core", swap) for part in parts]
    weight = padded_weight(place, embed_weight, parts)
    part = first_half(sends, arrived0, weight)
    grads, mine, send, sums = norm_backward(
        place, sends, arrived1, part, weight, grad_norm, grad_resid, norm_gain.reshape(1, D)
    )
    theirs = lax.ppermute(send, "core", swap)
    their_grads = lax.ppermute(grads, "core", swap)
    own, *sent = products(place, own_products(grads, mine, sums), their_grads, theirs)
    terms = [lax.ppermute(sent[by - 1], plane, plane_shift(by, 0)) for by in (1, 3, 2)]
    keep, *sent = fold(place, own, terms)
    terms = [lax.ppermute(sent[by - 1], plane, plane_shift(by, 1)) for by in (1, 3, 2)]
    quarter = keep + terms[0].astype(jnp.float32) + terms[1].astype(jnp.float32) + terms[2].astype(jnp.float32)
    quarter = jnp.pad(quarter, ((0, 8 * PIECE - QUARTER), (0, 0)))
    pieces = lax.all_to_all(quarter.reshape(8, PIECE, 128), "z", 0, 0, tiled=True)
    quarter = copies(jnp.sum(pieces, axis=0), "z", 8).reshape(8 * PIECE, 128)[:QUARTER]
    mine = [quarter] + [lax.ppermute(quarter, "slab", ring(by)) for by in (1, 2, 3)]
    return finish(place, mine + [lax.ppermute(part, "core", swap) for part in mine])


def solution(mesh):
    split = Mesh(mesh.devices.reshape(8, 2, 4, 4), ("z", "core", "slab", "fsdp"))
    dp = ("z", "core")
    return jax.shard_map(
        shards,
        mesh=split,
        in_specs=(
            P(dp, "fsdp", "slab", None, None, None),
            P("slab", "fsdp", dp, None),
            P("slab", "fsdp", dp, None),
            P("fsdp", None),
            P(),
            P("slab", "fsdp", dp),
            P("slab", "fsdp", dp),
        ),
        out_specs=(P("fsdp", None), P(None, "fsdp")),
        check_vma=False,
    )
```
